512 devices in a mesh: cells: 128 (over y, z, core), per: 4 (over x).
Axes of the slice: x: 4, y: 4, z: 16, core: 2. Of those that a mesh axis runs over, the one named last changes fastest.
Arguments:
- field: float32 [128, 2, 8, 65536], P('per', None, None, 'cells'), may hold values from -12 to 12
- period_gain: float32 [128], replicated, may hold values from 0.3 to 3
- start_basis: float32 [128, 32], replicated, may hold values from -0.5 to 0.5
Outputs:
- projected: float32 [128, 2, 8, 65536], P('per', None, None, 'cells')
The draws below stay inside these ranges and needn't reach their ends.
All inputs are finite; a program needn't handle non-finite values.
Results may differ from the reference program's by a relative error of at most 0.0003.
Values sent between devices are 32-bit elements; how exact they have to be, the bound alone decides.
No kernel may reach another device: no remote copies, remote signals or barrier semaphores. Data moves between devices by JAX's collectives and lax.ppermute only.
A program may use at most 192 MiB of HBM per device.

```python
import math
import jax
import jax.numpy as jnp
from jax import lax

PERIODS = 128
RANK = 32
LAYERS = 8
ITERS = 3
CELLS = 65536


def draw_field(key, part):
    key = jax.random.fold_in(key, 11)
    first = jax.random.fold_in(key, 0)
    second = jax.random.fold_in(key, 1)
    fourth = jax.random.fold_in(key, 3)
    fifth = jax.random.fold_in(key, 4)
    shape = (PERIODS, 2, LAYERS, CELLS)
    ramp = jnp.exp(jnp.log(3.0) * jnp.arange(CELLS, dtype=jnp.float32) / max(CELLS - 1, 1))
    rough = jnp.exp(jax.random.uniform(second, (CELLS,), minval=-0.7, maxval=0.7))
    position = (jnp.arange(PERIODS, dtype=jnp.float32) + 0.5) / PERIODS
    phases = jax.random.uniform(fourth, (16,), minval=0.0, maxval=2.0 * math.pi)
    weights = jax.random.normal(fifth, (16, 2, LAYERS, CELLS))
    common = jnp.zeros(shape, jnp.float32)
    for index in range(16):
        profile = jnp.cos(math.pi * (index + 0.5) * position + phases[index]) * math.sqrt(2.0 / 16.0)
        common = common + profile[:, None, None, None] * weights[index][None]
    base = jax.random.normal(first, shape)
    values = (base + common) * ramp * rough
    return jnp.clip(values, -12.0, 12.0).astype(jnp.float32)


def scatter_about(own_key, shape, scale, reach, kind=jnp.bfloat16):
    return jnp.clip(scale * jax.random.normal(own_key, shape, jnp.float32), -reach, reach).astype(kind)


def setup_inputs(seed: int = 0) -> dict:
    seeds = jax.random.split(jax.random.key(seed), 4)
    return {
        "field": draw_field(jax.random.fold_in(seeds[3], 71), 0),
        "period_gain": jnp.clip(jnp.exp(jax.random.uniform(seeds[1], (PERIODS,), jnp.float32, math.log(0.3), math.log(3.0))), 0.3, 3.0),
        "start_basis": scatter_about(seeds[2], (PERIODS, RANK), PERIODS ** -0.5, 0.5, jnp.float32),
    }


HIGH = lax.Precision.HIGHEST

def refine(gram, basis):
    for step in range(ITERS):
        grown = jnp.dot(gram, basis, precision=HIGH)
        inner = jnp.dot(grown.T, grown, precision=HIGH)
        lower = jnp.linalg.cholesky(inner)
        basis = lax.linalg.triangular_solve(lower, grown, left_side=False, lower=True, transpose_a=True)
    return basis

def reference(field, period_gain, start_basis):
    scaled = field * period_gain[:, None, None, None]
    flat = scaled.reshape(scaled.shape[0], -1)
    gram = lax.dot_general(flat, flat, (((1,), (1,)), ((), ())), precision=HIGH) / (2.0 * LAYERS * CELLS)
    basis = refine(gram, start_basis)
    projector = jnp.dot(basis, basis.T, precision=HIGH)
    result = lax.dot_general(projector, flat, (((0,), (0,)), ((), ())), precision=HIGH)
    return result.reshape(scaled.shape)
```

```python
import functools

import jax
import jax.numpy as jnp
from jax import lax
from jax.experimental import pallas as pl
from jax.experimental.pallas import tpu as pltpu
from jax.sharding import Mesh, PartitionSpec as P

ITERS = 3
HIGH = lax.Precision.HIGHEST
PLANE = ("y", "c", "x")
VMEM = pl.BlockSpec(memory_space=pltpu.VMEM)
ANY = pl.BlockSpec(memory_space=pl.ANY)


def dot(a, b, ca, cb):
    return lax.dot_general(
        a, b, (((ca,), (cb,)), ((), ())), precision=HIGH, preferred_element_type=jnp.float32
    )


def pack_kernel(groups, field_ref, out_ref, sems):
    width = field_ref.shape[3] // groups
    copies = [
        pltpu.make_async_copy(
            field_ref.at[:, :, :, pl.ds(g * width, width)], out_ref.at[g], sems.at[g]
        )
        for g in range(groups)
    ]
    for copy in copies:
        copy.start()
    for copy in copies:
        copy.wait()


def pack(field, groups):
    local, parts, layers, cells = field.shape
    return pl.pallas_call(
        functools.partial(pack_kernel, groups),
        out_shape=jax.ShapeDtypeStruct((groups, local, parts, layers, cells // groups), field.dtype),
        in_specs=[ANY],
        out_specs=VMEM,
        scratch_shapes=[pltpu.SemaphoreType.DMA((groups,))],
        name="pack",
    )(field)


def gram_kernel(rows_ref, out_ref):
    periods = out_ref.shape[0]
    per_period = rows_ref.shape[0] // periods
    acc = None
    for s in range(0, per_period, 2):
        block = jnp.concatenate(
            [rows_ref[pl.ds(s + t, periods, stride=per_period), :] for t in range(2)], axis=1
        )
        part = dot(block, block, 1, 1)
        acc = part if acc is None else acc + part
    out_ref[...] = acc


def gram_of(rows, periods):
    return pl.pallas_call(
        gram_kernel,
        out_shape=jax.ShapeDtypeStruct((periods, periods), jnp.float32),
        in_specs=[VMEM],
        out_specs=VMEM,
        name="gram",
    )(rows)


def inverse_factor(inner):
    rank = inner.shape[0]
    row = lax.broadcasted_iota(jnp.int32, (rank, rank), 0)
    col = lax.broadcasted_iota(jnp.int32, (rank, rank), 1)
    eye = jnp.where(row == col, 1.0, 0.0)
    work = jnp.concatenate([inner, eye], axis=1)
    sub = lax.broadcasted_iota(jnp.int32, (rank, 1), 0)
    pivots = jnp.ones((rank, 1), jnp.float32)
    for k in range(rank):
        column = work[:, k : k + 1]
        line = work[k : k + 1, :]
        pivot = line[:, k : k + 1]
        pivots = jnp.where(sub == k, pivot, pivots)
        if k + 1 < rank:
            factor = jnp.where(sub > k, column * (1.0 / pivot), 0.0)
            work = work - factor * line
    return work[:, rank:] * lax.rsqrt(pivots)


def refine_kernel(raw_ref, gain_row_ref, gain_col_ref, start_ref, group_ref, out_ref, full_ref, *, rows):
    local = out_ref.shape[0]
    gram = raw_ref[...] * (gain_col_ref[...] * gain_row_ref[...]) * (1.0 / rows)
    basis = start_ref[...]
    for _ in range(ITERS):
        grown = dot(basis, gram, 1, 0)
        basis = dot(inverse_factor(dot(grown, grown, 1, 1)), grown, 1, 0)
    full_ref[...] = dot(basis, basis, 0, 0) * gain_row_ref[...]
    out_ref[...] = full_ref[pl.ds(pl.multiple_of(group_ref[0] * local, local), local), :]


def refine(raw, gain, start_basis, group, local, rows):
    periods = raw.shape[0]
    return pl.pallas_call(
        functools.partial(refine_kernel, rows=rows),
        out_shape=jax.ShapeDtypeStruct((local, periods), jnp.float32),
        in_specs=[VMEM, VMEM, VMEM, VMEM, pl.BlockSpec(memory_space=pltpu.SMEM)],
        out_specs=VMEM,
        scratch_shapes=[pltpu.VMEM(raw.shape, jnp.float32)],
        name="refine",
    )(raw, gain[None, :], gain[:, None], start_basis.T, group[None])


def project_kernel(mix_ref, whole_ref, out_ref):
    mix = mix_ref[...]
    for layer in range(out_ref.shape[2]):
        out_ref[:, 0, layer, :] = dot(mix, whole_ref[:, 0, layer, :], 1, 0)


def project(mix, whole):
    local, periods = mix.shape
    _, parts, layers, cells = whole.shape
    width = cells // 2
    return pl.pallas_call(
        project_kernel,
        out_shape=jax.ShapeDtypeStruct((local, parts, layers, cells), jnp.float32),
        grid=(parts, cells // width),
        in_specs=[
            pl.BlockSpec((local, periods), lambda i, j: (0, 0)),
            pl.BlockSpec((periods, 1, layers, width), lambda i, j: (0, i, 0, j)),
        ],
        out_specs=pl.BlockSpec((local, 1, layers, width), lambda i, j: (0, i, 0, j)),
        name="project",
    )(mix, whole)


def spread(block, axes, count):
    copies = lax.optimization_barrier(jnp.broadcast_to(block[None], (count,) + block.shape))
    return lax.all_to_all(copies, axes, 0, 0, tiled=True)


def total(value):
    rows = value.shape[0]
    plane = lax.axis_size("y") * lax.axis_size("c") * lax.axis_size("x")
    pieces = lax.all_to_all(value.reshape(plane, rows // plane, -1), PLANE, 0, 0, tiled=True)
    piece = spread(jnp.sum(pieces, 0), "z", lax.axis_size("z"))
    return spread(jnp.sum(piece, 0), PLANE, plane).reshape(value.shape)


def per_device(field, gain, start_basis):
    groups = lax.axis_size("x")
    local, parts, layers, cells = field.shape
    periods = gain.shape[0]
    devices = lax.axis_size("y") * lax.axis_size("z") * lax.axis_size("c")
    total_rows = float(parts * layers * cells * devices)
    blocks = pack(field, groups).reshape(groups, -1, cells // groups)
    rows = lax.all_to_all(blocks, "x", 0, 0, tiled=True)
    later, rows = lax.optimization_barrier((field, rows))
    whole = lax.all_gather(later, "x", axis=0, tiled=True)
    raw = total(gram_of(rows.reshape(-1, cells // groups), periods))
    mix = refine(raw, gain, start_basis, lax.axis_index("x"), local, total_rows)
    return project(mix, whole)


def solution(mesh):
    cells, per = mesh.devices.shape
    split = Mesh(mesh.devices.reshape(4, cells // 8, 2, per), ("y", "z", "c", "x"))
    spec = P("x", None, None, ("y", "z", "c"))
    return jax.shard_map(
        per_device, mesh=split, in_specs=(spec, P(), P()), out_specs=spec, check_vma=False
    )
```

```python
import functools

import jax
import jax.numpy as jnp
from jax import lax
from jax.experimental import pallas as pl
from jax.experimental.pallas import tpu as pltpu
from jax.sharding import Mesh, PartitionSpec as P

ITERS = 3
PIVOTS = 4
HIGH = lax.Precision.HIGHEST
PLANE = ("y", "c", "x")
VMEM = pl.BlockSpec(memory_space=pltpu.VMEM)
ANY = pl.BlockSpec(memory_space=pl.ANY)


def dot(a, b, ca, cb, precision=HIGH):
    return lax.dot_general(
        a, b, (((ca,), (cb,)), ((), ())), precision=precision, preferred_element_type=jnp.float32
    )


def halves(value):
    high = value.astype(jnp.bfloat16)
    return high, (value - high.astype(jnp.float32)).astype(jnp.bfloat16)


def run_copies(copies):
    for copy in copies:
        copy.start()
    for copy in copies:
        copy.wait()


def pack_kernel(groups, field_ref, out_ref, sems):
    width = field_ref.shape[3] // groups
    run_copies([
        pltpu.make_async_copy(
            field_ref.at[:, :, :, pl.ds(g * width, width)], out_ref.at[g], sems.at[g]
        )
        for g in range(groups)
    ])


def pack(field, groups):
    local, parts, layers, cells = field.shape
    return pl.pallas_call(
        functools.partial(pack_kernel, groups),
        out_shape=jax.ShapeDtypeStruct((groups, local, parts, layers, cells // groups), field.dtype),
        in_specs=[ANY],
        out_specs=ANY,
        scratch_shapes=[pltpu.SemaphoreType.DMA((groups,))],
        name="pack",
    )(field)


def unpack_kernel(groups, blocks_ref, out_ref, sems):
    width = out_ref.shape[3] // groups
    run_copies([
        pltpu.make_async_copy(
            blocks_ref.at[g], out_ref.at[:, :, :, pl.ds(g * width, width)], sems.at[g]
        )
        for g in range(groups)
    ])


def unpack(blocks):
    groups, local, parts, layers, width = blocks.shape
    return pl.pallas_call(
        functools.partial(unpack_kernel, groups),
        out_shape=jax.ShapeDtypeStruct((local, parts, layers, groups * width), blocks.dtype),
        in_specs=[ANY],
        out_specs=ANY,
        scratch_shapes=[pltpu.SemaphoreType.DMA((groups,))],
        name="unpack",
    )(blocks)


def period_block(rows_ref, periods, s):
    per_period = rows_ref.shape[0] // periods
    return jnp.concatenate(
        [rows_ref[pl.ds(s + t, periods, stride=per_period), :] for t in range(2)], axis=1
    )


def gram_kernel(rows_ref, out_ref):
    periods = out_ref.shape[0]
    acc = None
    for s in range(0, rows_ref.shape[0] // periods, 2):
        both = jnp.concatenate(halves(period_block(rows_ref, periods, s)), axis=0)
        part = dot(both, both, 1, 1, None)
        acc = part if acc is None else acc + part
    cross = acc[:periods, periods:] + acc[periods:, :periods]
    out_ref[...] = acc[:periods, :periods] + (cross + acc[periods:, periods:])


def gram_of(rows, periods):
    return pl.pallas_call(
        gram_kernel,
        out_shape=jax.ShapeDtypeStruct((periods, periods), jnp.float32),
        in_specs=[VMEM],
        out_specs=VMEM,
        name="gram",
    )(rows)


def inverse_factor(inner):
    rank = inner.shape[0]
    row = lax.broadcasted_iota(jnp.int32, (rank, rank), 0)
    col = lax.broadcasted_iota(jnp.int32, (rank, rank), 1)
    work = jnp.concatenate([inner, jnp.where(row == col, 1.0, 0.0)], axis=1)
    shape = work.shape
    sub = lax.broadcasted_iota(jnp.int32, shape, 0)
    pivots = jnp.ones(shape, jnp.float32)
    for start in range(0, rank, PIVOTS):
        ks = range(start, start + PIVOTS)
        columns = [jnp.broadcast_to(work[:, k : k + 1], shape) for k in ks]
        lines = [work[k : k + 1, :] for k in ks]
        for j, k in enumerate(ks):
            pivot = columns[j][k : k + 1, :]
            pivots = jnp.where(sub == k, pivot, pivots)
            factor = jnp.where(sub > k, columns[j] * (1.0 / pivot), 0.0)
            for i in range(j + 1, PIVOTS):
                columns[i] = columns[i] - factor * columns[i][k : k + 1, :]
                lines[i] = lines[i] - factor[start + i : start + i + 1, :] * lines[j]
            work = work - factor * lines[j]
    return work[:, rank:] * lax.rsqrt(pivots[:, rank:])


def project_kernel(count, raw_ref, gain_ref, start_ref, rows_ref, out_ref, held, sem):
    fetch = pltpu.make_async_copy(rows_ref, held, sem)
    fetch.start()
    raw = raw_ref[...]
    gain = gain_ref[...]
    periods = raw.shape[0]

    def grow(basis):
        return dot(basis * gain, raw, 1, 0) * (gain * (1.0 / count))

    grown = grow(start_ref[...])
    for _ in range(ITERS - 1):
        later = grow(grown)
        grown = dot(inverse_factor(dot(grown, grown, 1, 1)), later, 1, 0)
    basis = dot(inverse_factor(dot(grown, grown, 1, 1)), grown, 1, 0)
    mix_high, mix_low = halves(dot(basis, basis, 0, 0) * gain)
    fetch.wait()
    per_period = held.shape[0] // periods
    width = held.shape[1]
    for s in range(0, per_period, 2):
        high, low = halves(period_block(held, periods, s))
        result = dot(mix_high, high, 1, 0, None) + (
            dot(mix_high, low, 1, 0, None) + dot(mix_low, high, 1, 0, None)
        )
        for t in range(2):
            out_ref[pl.ds(s + t, periods, stride=per_period), :] = result[:, t * width : (t + 1) * width]


def project(raw, gain, start_basis, rows, count):
    return pl.pallas_call(
        functools.partial(project_kernel, count),
        out_shape=jax.ShapeDtypeStruct(rows.shape, jnp.float32),
        in_specs=[VMEM, VMEM, VMEM, ANY],
        out_specs=VMEM,
        scratch_shapes=[pltpu.VMEM(rows.shape, jnp.float32), pltpu.SemaphoreType.DMA(())],
        name="project",
    )(raw, gain[None, :], start_basis.T, rows)


def spread(block, axes, count):
    copies = lax.optimization_barrier(jnp.broadcast_to(block[None], (count,) + block.shape))
    return lax.all_to_all(copies, axes, 0, 0, tiled=True)


def total(value):
    rows = value.shape[0]
    plane = lax.axis_size("y") * lax.axis_size("c") * lax.axis_size("x")
    pieces = lax.all_to_all(value.reshape(plane, rows // plane, -1), PLANE, 0, 0, tiled=True)
    piece = spread(jnp.sum(pieces, 0), "z", lax.axis_size("z"))
    return spread(jnp.sum(piece, 0), PLANE, plane).reshape(value.shape)


def per_device(field, gain, start_basis):
    groups = lax.axis_size("x")
    local, parts, layers, cells = field.shape
    periods = gain.shape[0]
    devices = lax.axis_size("y") * lax.axis_size("z") * lax.axis_size("c")
    count = float(parts * layers * cells * devices)
    width = cells // groups
    blocks = pack(field, groups).reshape(groups, -1, width)
    rows = lax.all_to_all(blocks, "x", 0, 0, tiled=True).reshape(-1, width)
    raw = total(gram_of(rows, periods))
    result = project(raw, gain, start_basis, rows, count).reshape(groups, -1, width)
    result = lax.all_to_all(result, "x", 0, 0, tiled=True)
    return unpack(result.reshape(groups, local, parts, layers, width))


def solution(mesh):
    cells, per = mesh.devices.shape
    split = Mesh(mesh.devices.reshape(4, cells // 8, 2, per), ("y", "z", "c", "x"))
    spec = P("x", None, None, ("y", "z", "c"))
    return jax.shard_map(
        per_device, mesh=split, in_specs=(spec, P(), P()), out_specs=spec, check_vma=False
    )
```

```python
import functools

import jax
import jax.numpy as jnp
from jax import lax
from jax.experimental import pallas as pl
from jax.experimental.pallas import tpu as pltpu
from jax.sharding import Mesh, PartitionSpec as P

ITERS = 3
PIVOTS = 4
LANES = 128
HIGH = lax.Precision.HIGHEST
PLANE = ("y", "c", "x")
VMEM = pl.BlockSpec(memory_space=pltpu.VMEM)
ANY = pl.BlockSpec(memory_space=pl.ANY)


def dot(a, b, ca, cb, precision=HIGH):
    return lax.dot_general(
        a, b, (((ca,), (cb,)), ((), ())), precision=precision, preferred_element_type=jnp.float32
    )


def halves(value):
    high = value.astype(jnp.bfloat16)
    return high, (value - high.astype(jnp.float32)).astype(jnp.bfloat16)


def run_copies(copies):
    for copy in copies:
        copy.start()
    for copy in copies:
        copy.wait()


def pack_kernel(groups, field_ref, out_ref, sems):
    width = field_ref.shape[3] // groups
    run_copies([
        pltpu.make_async_copy(
            field_ref.at[:, :, :, pl.ds(g * width, width)], out_ref.at[g], sems.at[g]
        )
        for g in range(groups)
    ])


def pack(field, groups):
    local, parts, layers, cells = field.shape
    return pl.pallas_call(
        functools.partial(pack_kernel, groups),
        out_shape=jax.ShapeDtypeStruct((groups, local, parts, layers, cells // groups), field.dtype),
        in_specs=[ANY],
        out_specs=VMEM,
        scratch_shapes=[pltpu.SemaphoreType.DMA((groups,))],
        name="pack",
    )(field)


def period_block(rows_ref, periods, s):
    per_period = rows_ref.shape[0] // periods
    return jnp.concatenate(
        [rows_ref[pl.ds(s + t, periods, stride=per_period), :] for t in range(2)], axis=1
    )


def gram_kernel(rows_ref, out_ref):
    periods = out_ref.shape[0]
    acc = None
    for s in range(0, rows_ref.shape[0] // periods, 2):
        both = jnp.concatenate(halves(period_block(rows_ref, periods, s)), axis=0)
        part = dot(both, both, 1, 1, None)
        acc = part if acc is None else acc + part
    cross = acc[:periods, periods:] + acc[periods:, :periods]
    out_ref[...] = acc[:periods, :periods] + (cross + acc[periods:, periods:])


def gram_of(rows, periods):
    return pl.pallas_call(
        gram_kernel,
        out_shape=jax.ShapeDtypeStruct((periods, periods), jnp.float32),
        in_specs=[VMEM],
        out_specs=VMEM,
        name="gram",
    )(rows)


def inverse_factor(inner):
    rank = inner.shape[0]
    row = lax.broadcasted_iota(jnp.int32, (rank, rank), 0)
    col = lax.broadcasted_iota(jnp.int32, (rank, rank), 1)
    work = jnp.concatenate([inner, jnp.where(row == col, 1.0, 0.0)], axis=1)
    shape = work.shape
    sub = lax.broadcasted_iota(jnp.int32, shape, 0)
    pivots = jnp.ones(shape, jnp.float32)
    for start in range(0, rank, PIVOTS):
        ks = range(start, start + PIVOTS)
        columns = [jnp.broadcast_to(work[:, k : k + 1], shape) for k in ks]
        lines = [work[k : k + 1, :] for k in ks]
        for j, k in enumerate(ks):
            pivot = columns[j][k : k + 1, :]
            pivots = jnp.where(sub == k, pivot, pivots)
            factor = jnp.where(sub > k, columns[j] * (1.0 / pivot), 0.0)
            for i in range(j + 1, PIVOTS):
                columns[i] = columns[i] - factor * columns[i][k : k + 1, :]
                lines[i] = lines[i] - factor[start + i : start + i + 1, :] * lines[j]
            work = work - factor * lines[j]
    return work[:, rank:] * lax.rsqrt(pivots[:, rank:])


def project_kernel(count, raw_ref, gain_ref, start_ref, group_ref, *refs):
    blocks, (out_ref, held, ready, full_ref, in_sems, out_sems) = refs[:-6], refs[-6:]
    height, cells = out_ref.shape
    lanes = held.shape[1]
    tiles = cells // lanes
    rows = held.shape[0] // tiles
    fetches, at = [], 0
    for block in blocks:
        for c in range(tiles):
            fetches.append(
                pltpu.make_async_copy(
                    block.at[:, pl.ds(c * lanes, lanes)],
                    held.at[pl.ds(c * rows + at, block.shape[0])],
                    in_sems.at[len(fetches)],
                )
            )
        at += block.shape[0]
    for fetch in fetches:
        fetch.start()
    raw = raw_ref[...]
    gain = gain_ref[...]
    periods = raw.shape[0]
    per_period = rows // periods
    local = height // per_period

    def grow(basis):
        return dot(basis * gain, raw, 1, 0) * (gain * (1.0 / count))

    grown = grow(start_ref[...])
    for _ in range(ITERS - 1):
        later = grow(grown)
        grown = dot(inverse_factor(dot(grown, grown, 1, 1)), later, 1, 0)
    basis = dot(inverse_factor(dot(grown, grown, 1, 1)), grown, 1, 0)
    full_ref[...] = dot(basis, basis, 0, 0) * gain
    first = group_ref[0] * local
    own = full_ref[pl.ds(pl.multiple_of(first, local), local), :]
    high, low = halves(pltpu.roll(own, lax.rem(periods - first, periods), 1))
    mix = jnp.concatenate(
        [jnp.concatenate([high, high], axis=1), jnp.concatenate([low, jnp.zeros_like(low)], axis=1)],
        axis=0,
    )
    for fetch in fetches:
        fetch.wait()
    sends = []
    for pair in range(0, tiles, 2):
        for s in range(per_period):
            line = jnp.concatenate(
                [
                    held[pl.ds(c * rows + s, periods, stride=per_period), :]
                    for c in range(pair, pair + 2)
                ],
                axis=1,
            )
            result = dot(mix, jnp.concatenate(halves(line), axis=0), 1, 0, None)
            result = result[:local] + result[local:]
            for c in range(2):
                ready[pl.ds((pair + c) * height + s, local, stride=per_period), :] = result[
                    :, c * lanes : (c + 1) * lanes
                ]
        for c in range(pair, pair + 2):
            sends.append(
                pltpu.make_async_copy(
                    ready.at[pl.ds(c * height, height)],
                    out_ref.at[:, pl.ds(c * lanes, lanes)],
                    out_sems.at[c],
                )
            )
            sends[-1].start()
    for send in sends:
        send.wait()


def project(raw, gain, start_basis, group, blocks, count):
    rows = sum(block.shape[0] for block in blocks)
    tiles = blocks[0].shape[1] // LANES
    return pl.pallas_call(
        functools.partial(project_kernel, count),
        out_shape=jax.ShapeDtypeStruct(blocks[0].shape, jnp.float32),
        in_specs=[VMEM, VMEM, VMEM, pl.BlockSpec(memory_space=pltpu.SMEM)] + [ANY] * len(blocks),
        out_specs=ANY,
        scratch_shapes=[
            pltpu.VMEM((tiles * rows, LANES), jnp.float32),
            pltpu.VMEM((tiles * blocks[0].shape[0], LANES), jnp.float32),
            pltpu.VMEM(raw.shape, jnp.float32),
            pltpu.SemaphoreType.DMA((len(blocks) * tiles,)),
            pltpu.SemaphoreType.DMA((tiles,)),
        ],
        compiler_params=pltpu.CompilerParams(vmem_limit_bytes=32 * 2**20),
        name="project",
    )(raw, gain[None, :], start_basis.T, group[None], *blocks)


def spread(block, axes, count):
    copies = lax.optimization_barrier(jnp.broadcast_to(block[None], (count,) + block.shape))
    return lax.all_to_all(copies, axes, 0, 0, tiled=True)


def shift(value, step):
    count = lax.axis_size("x")
    return lax.ppermute(value, "x", [(i, (i + step) % count) for i in range(count)])


def per_device(field, gain, start_basis):
    groups = lax.axis_size("x")
    local, parts, layers, cells = field.shape
    periods = gain.shape[0]
    devices = lax.axis_size("y") * lax.axis_size("z") * lax.axis_size("c")
    plane = lax.axis_size("y") * lax.axis_size("c") * groups
    count = float(parts * layers * cells * devices)
    width = cells // groups
    blocks = pack(field, groups).reshape(groups, -1, width)
    rows = lax.all_to_all(blocks, "x", 0, 0, tiled=True)
    own, rows = lax.optimization_barrier((field.reshape(-1, cells), rows))
    before = shift(own, 1)
    after = shift(own, -1)
    gram = gram_of(rows.reshape(-1, width), periods)
    pieces = lax.all_to_all(gram.reshape(plane, periods // plane, -1), PLANE, 0, 0, tiled=True)
    piece = jnp.sum(spread(jnp.sum(pieces, 0), "z", lax.axis_size("z")), 0)
    before, after, piece = lax.optimization_barrier((before, after, piece))
    half = own.shape[0] // 2
    opposite = [shift(before[:half], 1), shift(after[half:], -1)]
    raw = spread(piece, PLANE, plane).reshape(gram.shape)
    blocks = [own, after, *opposite, before]
    result = project(raw, gain, start_basis, lax.axis_index("x"), blocks, count)
    return result.reshape(field.shape)


def solution(mesh):
    cells, per = mesh.devices.shape
    split = Mesh(mesh.devices.reshape(4, cells // 8, 2, per), ("y", "z", "c", "x"))
    spec = P("x", None, None, ("y", "z", "c"))
    return jax.shard_map(
        per_device, mesh=split, in_specs=(spec, P(), P()), out_specs=spec, check_vma=False
    )
```

```python
import functools

import jax
import jax.numpy as jnp
from jax import lax
from jax.experimental import pallas as pl
from jax.experimental.pallas import tpu as pltpu
from jax.sharding import Mesh, PartitionSpec as P

ITERS = 3
PIVOTS = 4
LANES = 128
HIGH = lax.Precision.HIGHEST
PAIRS = ("y", "c")
VMEM = pl.BlockSpec(memory_space=pltpu.VMEM)
ANY = pl.BlockSpec(memory_space=pl.ANY)


def dot(a, b, ca, cb, precision=HIGH):
    return lax.dot_general(
        a, b, (((ca,), (cb,)), ((), ())), precision=precision, preferred_element_type=jnp.float32
    )


def halves(value):
    high = value.astype(jnp.bfloat16)
    return high, (value - high.astype(jnp.float32)).astype(jnp.bfloat16)


def run_copies(copies):
    for copy in copies:
        copy.start()
    for copy in copies:
        copy.wait()


def pack_kernel(groups, field_ref, out_ref, sems):
    width = field_ref.shape[3] // groups
    run_copies([
        pltpu.make_async_copy(
            field_ref.at[:, :, :, pl.ds(g * width, width)], out_ref.at[g], sems.at[g]
        )
        for g in range(groups)
    ])


def pack(field, groups):
    local, parts, layers, cells = field.shape
    return pl.pallas_call(
        functools.partial(pack_kernel, groups),
        out_shape=jax.ShapeDtypeStruct((groups, local, parts, layers, cells // groups), field.dtype),
        in_specs=[ANY],
        out_specs=VMEM,
        scratch_shapes=[pltpu.SemaphoreType.DMA((groups,))],
        name="pack",
    )(field)


def period_block(rows_ref, periods, s):
    per_period = rows_ref.shape[0] // periods
    return jnp.concatenate(
        [rows_ref[pl.ds(s + t, periods, stride=per_period), :] for t in range(2)], axis=1
    )


def gram_kernel(rows_ref, out_ref):
    periods = out_ref.shape[0]
    acc = None
    for s in range(0, rows_ref.shape[0] // periods, 2):
        both = jnp.concatenate(halves(period_block(rows_ref, periods, s)), axis=0)
        part = dot(both, both, 1, 1, None)
        acc = part if acc is None else acc + part
    cross = acc[:periods, periods:] + acc[periods:, :periods]
    out_ref[...] = acc[:periods, :periods] + (cross + acc[periods:, periods:])


def gram_of(rows, periods):
    return pl.pallas_call(
        gram_kernel,
        out_shape=jax.ShapeDtypeStruct((periods, periods), jnp.float32),
        in_specs=[VMEM],
        out_specs=VMEM,
        name="gram",
    )(rows)


def inverse_factor(inner):
    rank = inner.shape[0]
    row = lax.broadcasted_iota(jnp.int32, (rank, rank), 0)
    col = lax.broadcasted_iota(jnp.int32, (rank, rank), 1)
    work = jnp.concatenate([inner, jnp.where(row == col, 1.0, 0.0)], axis=1)
    shape = work.shape
    sub = lax.broadcasted_iota(jnp.int32, shape, 0)
    pivots = jnp.ones(shape, jnp.float32)
    for start in range(0, rank, PIVOTS):
        ks = range(start, start + PIVOTS)
        columns = [jnp.broadcast_to(work[:, k : k + 1], shape) for k in ks]
        lines = [work[k : k + 1, :] for k in ks]
        for j, k in enumerate(ks):
            pivot = columns[j][k : k + 1, :]
            pivots = jnp.where(sub == k, pivot, pivots)
            factor = jnp.where(sub > k, columns[j] * (1.0 / pivot), 0.0)
            for i in range(j + 1, PIVOTS):
                columns[i] = columns[i] - factor * columns[i][k : k + 1, :]
                lines[i] = lines[i] - factor[start + i : start + i + 1, :] * lines[j]
            work = work - factor * lines[j]
    return work[:, rank:] * lax.rsqrt(pivots[:, rank:])


def project_kernel(count, raw_ref, gain_ref, start_ref, group_ref, *refs):
    blocks, (out_ref, held, ready, full_ref, in_sems, out_sems) = refs[:-6], refs[-6:]
    height, cells = out_ref.shape
    lanes = held.shape[1]
    tiles = cells // lanes
    rows = held.shape[0] // tiles
    fetches, at = [], 0
    for block in blocks:
        for c in range(tiles):
            fetches.append(
                pltpu.make_async_copy(
                    block.at[:, pl.ds(c * lanes, lanes)],
                    held.at[pl.ds(c * rows + at, block.shape[0])],
                    in_sems.at[len(fetches)],
                )
            )
        at += block.shape[0]
    for fetch in fetches:
        fetch.start()
    periods = raw_ref.shape[1]
    raw = sum(raw_ref[pl.ds(at, periods), :] for at in range(0, raw_ref.shape[0], periods))
    gain = gain_ref[...]
    per_period = rows // periods
    local = height // per_period

    def grow(basis):
        return dot(basis * gain, raw, 1, 0) * (gain * (1.0 / count))

    grown = grow(start_ref[...])
    for _ in range(ITERS - 1):
        later = grow(grown)
        grown = dot(inverse_factor(dot(grown, grown, 1, 1)), later, 1, 0)
    basis = dot(inverse_factor(dot(grown, grown, 1, 1)), grown, 1, 0)
    full_ref[...] = dot(basis, basis, 0, 0) * gain
    first = group_ref[0] * local
    own = full_ref[pl.ds(pl.multiple_of(first, local), local), :]
    high, low = halves(pltpu.roll(own, lax.rem(periods - first, periods), 1))
    mix = jnp.concatenate(
        [jnp.concatenate([high, high], axis=1), jnp.concatenate([low, jnp.zeros_like(low)], axis=1)],
        axis=0,
    )
    for fetch in fetches:
        fetch.wait()
    sends = []
    for pair in range(0, tiles, 2):
        for s in range(per_period):
            line = jnp.concatenate(
                [
                    held[pl.ds(c * rows + s, periods, stride=per_period), :]
                    for c in range(pair, pair + 2)
                ],
                axis=1,
            )
            result = dot(mix, jnp.concatenate(halves(line), axis=0), 1, 0, None)
            result = result[:local] + result[local:]
            for c in range(2):
                ready[pl.ds((pair + c) * height + s, local, stride=per_period), :] = result[
                    :, c * lanes : (c + 1) * lanes
                ]
        for c in range(pair, pair + 2):
            sends.append(
                pltpu.make_async_copy(
                    ready.at[pl.ds(c * height, height)],
                    out_ref.at[:, pl.ds(c * lanes, lanes)],
                    out_sems.at[c],
                )
            )
            sends[-1].start()
    for send in sends:
        send.wait()


def project(raw, gain, start_basis, group, blocks, count):
    rows = sum(block.shape[0] for block in blocks)
    tiles = blocks[0].shape[1] // LANES
    return pl.pallas_call(
        functools.partial(project_kernel, count),
        out_shape=jax.ShapeDtypeStruct(blocks[0].shape, jnp.float32),
        in_specs=[VMEM, VMEM, VMEM, pl.BlockSpec(memory_space=pltpu.SMEM)] + [ANY] * len(blocks),
        out_specs=ANY,
        scratch_shapes=[
            pltpu.VMEM((tiles * rows, LANES), jnp.float32),
            pltpu.VMEM((tiles * blocks[0].shape[0], LANES), jnp.float32),
            pltpu.VMEM((raw.shape[1], raw.shape[1]), jnp.float32),
            pltpu.SemaphoreType.DMA((len(blocks) * tiles,)),
            pltpu.SemaphoreType.DMA((tiles,)),
        ],
        compiler_params=pltpu.CompilerParams(vmem_limit_bytes=32 * 2**20),
        name="project",
    )(raw, gain[None, :], start_basis.T, group[None], *blocks)


def spread(block, axes, count):
    copies = lax.optimization_barrier(jnp.broadcast_to(block[None], (count,) + block.shape))
    return lax.all_to_all(copies, axes, 0, 0, tiled=True)


def shift(value, step):
    count = lax.axis_size("x")
    return lax.ppermute(value, "x", [(i, (i + step) % count) for i in range(count)])


def per_device(field, gain, start_basis):
    groups = lax.axis_size("x")
    local, parts, layers, cells = field.shape
    periods = gain.shape[0]
    devices = lax.axis_size("y") * lax.axis_size("z") * lax.axis_size("c")
    pairs = lax.axis_size("y") * lax.axis_size("c")
    count = float(parts * layers * cells * devices)
    width = cells // groups
    blocks = pack(field, groups).reshape(groups, -1, width)
    rows = lax.all_to_all(blocks, "x", 0, 0, tiled=True)
    own, rows = lax.optimization_barrier((field.reshape(-1, cells), rows))
    before = shift(own, 1)
    after = shift(own, -1)
    gram = gram_of(rows.reshape(-1, width), periods)
    pieces = lax.all_to_all(gram.reshape(pairs, periods // pairs, -1), PAIRS, 0, 0, tiled=True)
    piece = jnp.sum(spread(jnp.sum(pieces, 0), "z", lax.axis_size("z")), 0)
    half = own.shape[0] // 2
    opposite = [shift(before[:half], 1), shift(after[half:], -1)]
    raw = spread(piece, ("x",) + PAIRS, groups * pairs).reshape(-1, periods)
    blocks = [own, after, *opposite, before]
    result = project(raw, gain, start_basis, lax.axis_index("x"), blocks, count)
    return result.reshape(field.shape)


def solution(mesh):
    cells, per = mesh.devices.shape
    split = Mesh(mesh.devices.reshape(4, cells // 8, 2, per), ("y", "z", "c", "x"))
    spec = P("x", None, None, ("y", "z", "c"))
    return jax.shard_map(
        per_device, mesh=split, in_specs=(spec, P(), P()), out_specs=spec, check_vma=False
    )
```

```python
import functools

import jax
import jax.numpy as jnp
from jax import lax
from jax.experimental import pallas as pl
from jax.experimental.pallas import tpu as pltpu
from jax.sharding import Mesh, PartitionSpec as P

ITERS = 3
PIVOTS = 4
LANES = 128
EXTRA = 8
HIGH = lax.Precision.HIGHEST
PAIRS = ("y", "c")
VMEM = pl.BlockSpec(memory_space=pltpu.VMEM)
ANY = pl.BlockSpec(memory_space=pl.ANY)
LONG = pl.CostEstimate(flops=4 * 10**10, bytes_accessed=0, transcendentals=0)


def dot(a, b, ca, cb, precision=HIGH):
    return lax.dot_general(
        a, b, (((ca,), (cb,)), ((), ())), precision=precision, preferred_element_type=jnp.float32
    )


def halves(value):
    high = value.astype(jnp.bfloat16)
    return high, (value - high.astype(jnp.float32)).astype(jnp.bfloat16)


def run_copies(copies):
    for copy in copies:
        copy.start()
    for copy in copies:
        copy.wait()


def pack_kernel(groups, field_ref, out_ref, sems):
    width = field_ref.shape[3] // groups
    run_copies([
        pltpu.make_async_copy(
            field_ref.at[:, :, :, pl.ds(g * width, width)], out_ref.at[g], sems.at[g]
        )
        for g in range(groups)
    ])


def pack(field, groups):
    local, parts, layers, cells = field.shape
    return pl.pallas_call(
        functools.partial(pack_kernel, groups),
        out_shape=jax.ShapeDtypeStruct((groups, local, parts, layers, cells // groups), field.dtype),
        in_specs=[ANY],
        out_specs=VMEM,
        scratch_shapes=[pltpu.SemaphoreType.DMA((groups,))],
        name="pack",
    )(field)


def positions(shape):
    return lax.broadcasted_iota(jnp.int32, shape, 0), lax.broadcasted_iota(jnp.int32, shape, 1)


def period_block(rows_ref, periods, s):
    per_period = rows_ref.shape[0] // periods
    return jnp.concatenate(
        [rows_ref[pl.ds(s + t, periods, stride=per_period), :] for t in range(2)], axis=1
    )


def gram_kernel(rows_ref, out_ref):
    periods = out_ref.shape[1]
    acc = None
    for s in range(0, rows_ref.shape[0] // periods, 2):
        both = jnp.concatenate(halves(period_block(rows_ref, periods, s)), axis=0)
        part = dot(both, both, 1, 1, None)
        acc = part if acc is None else acc + part
    cross = acc[:periods, periods:] + acc[periods:, :periods]
    gram = acc[:periods, :periods] + (cross + acc[periods:, periods:])
    half = periods // 2
    low = gram[half:]
    row, lane = positions(low.shape)
    folded = jnp.where(row >= lane - half, pltpu.roll(gram[:half], half, 1), low)
    out_ref[:half] = jnp.where(lane < half, low, folded)
    corner = jnp.sum(jnp.where(row == lane - half, low, 0.0), axis=0, keepdims=True)
    out_ref[half:] = jnp.broadcast_to(corner, (EXTRA, periods))


def unfold(packed):
    periods = packed.shape[1]
    half = periods // 2
    body = packed[:half]
    row, lane = positions(body.shape)
    high = jnp.where(row >= lane, pltpu.roll(body, half, 1), 0.0)
    high = jnp.where(lane < half, high, 0.0) * jnp.where(row == lane, 0.5, 1.0)
    low = jnp.where((lane < half) | (row < lane - half), body, 0.0)
    low = jnp.where(row == lane - half, 0.5 * packed[half : half + 1], low)
    triangle = jnp.concatenate([high, low], axis=0)
    return triangle + triangle.T


def gram_of(rows, periods):
    return pl.pallas_call(
        gram_kernel,
        out_shape=jax.ShapeDtypeStruct((periods // 2 + EXTRA, periods), jnp.float32),
        in_specs=[VMEM],
        out_specs=VMEM,
        name="gram",
    )(rows)


def inverse_factor(inner):
    rank = inner.shape[0]
    row = lax.broadcasted_iota(jnp.int32, (rank, rank), 0)
    col = lax.broadcasted_iota(jnp.int32, (rank, rank), 1)
    work = jnp.concatenate([inner, jnp.where(row == col, 1.0, 0.0)], axis=1)
    shape = work.shape
    sub = lax.broadcasted_iota(jnp.int32, shape, 0)
    pivots = jnp.ones(shape, jnp.float32)
    for start in range(0, rank, PIVOTS):
        ks = range(start, start + PIVOTS)
        columns = [jnp.broadcast_to(work[:, k : k + 1], shape) for k in ks]
        lines = [work[k : k + 1, :] for k in ks]
        for j, k in enumerate(ks):
            pivot = columns[j][k : k + 1, :]
            pivots = jnp.where(sub == k, pivot, pivots)
            factor = jnp.where(sub > k, columns[j] * (1.0 / pivot), 0.0)
            for i in range(j + 1, PIVOTS):
                columns[i] = columns[i] - factor * columns[i][k : k + 1, :]
                lines[i] = lines[i] - factor[start + i : start + i + 1, :] * lines[j]
            work = work - factor * lines[j]
    return work[:, rank:] * lax.rsqrt(pivots[:, rank:])


def refine_kernel(count, raw_ref, gain_ref, start_ref, group_ref, out_ref, full_ref):
    periods = raw_ref.shape[1]
    local = out_ref.shape[0]
    size = periods // 2 + EXTRA
    raw = unfold(sum(raw_ref[pl.ds(at, size), :] for at in range(0, raw_ref.shape[0], size)))
    gain = gain_ref[...]

    def grow(basis):
        return dot(basis * gain, raw, 1, 0) * (gain * (1.0 / count))

    grown = grow(start_ref[...])
    for _ in range(ITERS - 1):
        later = grow(grown)
        grown = dot(inverse_factor(dot(grown, grown, 1, 1)), later, 1, 0)
    basis = dot(inverse_factor(dot(grown, grown, 1, 1)), grown, 1, 0)
    full_ref[...] = dot(basis, basis, 0, 0) * gain
    first = group_ref[0] * local
    own = full_ref[pl.ds(pl.multiple_of(first, local), local), :]
    out_ref[...] = pltpu.roll(own, lax.rem(periods - first, periods), 1)


def refine(raw, gain, start_basis, group, local, count):
    periods = gain.shape[0]
    return pl.pallas_call(
        functools.partial(refine_kernel, count),
        out_shape=jax.ShapeDtypeStruct((local, periods), jnp.float32),
        in_specs=[VMEM, VMEM, VMEM, pl.BlockSpec(memory_space=pltpu.SMEM)],
        out_specs=VMEM,
        scratch_shapes=[pltpu.VMEM((periods, periods), jnp.float32)],
        cost_estimate=LONG,
        name="refine",
    )(raw, gain[None, :], start_basis.T, group[None])


def project_kernel(mix_ref, *refs):
    blocks, (out_ref, held, ready, in_sems, out_sems) = refs[:-5], refs[-5:]
    height, cells = out_ref.shape
    lanes = held.shape[1]
    tiles = cells // lanes
    rows = held.shape[0] // tiles
    fetches = []
    for c in range(tiles):
        at = 0
        for block in blocks:
            fetches.append(
                pltpu.make_async_copy(
                    block.at[:, pl.ds(c * lanes, lanes)],
                    held.at[pl.ds(c * rows + at, block.shape[0])],
                    in_sems.at[len(fetches)],
                )
            )
            at += block.shape[0]
    for fetch in fetches:
        fetch.start()
    local, periods = mix_ref.shape
    per_period = rows // periods
    high, low = halves(mix_ref[...])
    mix = jnp.concatenate(
        [jnp.concatenate([high, high], axis=1), jnp.concatenate([low, jnp.zeros_like(low)], axis=1)],
        axis=0,
    )
    sends = []
    for pair in range(0, tiles, 2):
        for fetch in fetches[pair * len(blocks) : (pair + 2) * len(blocks)]:
            fetch.wait()
        for s in range(per_period):
            line = jnp.concatenate(
                [
                    held[pl.ds(c * rows + s, periods, stride=per_period), :]
                    for c in range(pair, pair + 2)
                ],
                axis=1,
            )
            result = dot(mix, jnp.concatenate(halves(line), axis=0), 1, 0, None)
            result = result[:local] + result[local:]
            for c in range(2):
                ready[pl.ds((pair + c) * height + s, local, stride=per_period), :] = result[
                    :, c * lanes : (c + 1) * lanes
                ]
        for c in range(pair, pair + 2):
            sends.append(
                pltpu.make_async_copy(
                    ready.at[pl.ds(c * height, height)],
                    out_ref.at[:, pl.ds(c * lanes, lanes)],
                    out_sems.at[c],
                )
            )
            sends[-1].start()
    for send in sends:
        send.wait()


def project(mix, blocks):
    rows = sum(block.shape[0] for block in blocks)
    tiles = blocks[0].shape[1] // LANES
    return pl.pallas_call(
        project_kernel,
        out_shape=jax.ShapeDtypeStruct(blocks[0].shape, jnp.float32),
        in_specs=[VMEM] + [ANY] * len(blocks),
        out_specs=ANY,
        scratch_shapes=[
            pltpu.VMEM((tiles * rows, LANES), jnp.float32),
            pltpu.VMEM((tiles * blocks[0].shape[0], LANES), jnp.float32),
            pltpu.SemaphoreType.DMA((len(blocks) * tiles,)),
            pltpu.SemaphoreType.DMA((tiles,)),
        ],
        compiler_params=pltpu.CompilerParams(vmem_limit_bytes=32 * 2**20),
        name="project",
    )(mix, *blocks)


def sum_kernel(pieces_ref, out_ref):
    piece = pieces_ref[0]
    for i in range(1, pieces_ref.shape[0]):
        piece = piece + pieces_ref[i]
    for i in range(out_ref.shape[0]):
        out_ref[i] = piece


def sum_and_copy(pieces, copies, cost):
    return pl.pallas_call(
        sum_kernel,
        out_shape=jax.ShapeDtypeStruct((copies,) + pieces.shape[1:], jnp.float32),
        in_specs=[VMEM],
        out_specs=VMEM,
        cost_estimate=cost,
        name="sum_and_copy",
    )(pieces)


def shift(value, step):
    count = lax.axis_size("x")
    return lax.ppermute(value, "x", [(i, (i + step) % count) for i in range(count)])


def per_device(field, gain, start_basis):
    groups = lax.axis_size("x")
    local, parts, layers, cells = field.shape
    periods = gain.shape[0]
    devices = lax.axis_size("y") * lax.axis_size("z") * lax.axis_size("c")
    pairs = lax.axis_size("y") * lax.axis_size("c")
    count = float(parts * layers * cells * devices)
    width = cells // groups
    blocks = pack(field, groups).reshape(groups, -1, width)
    rows = lax.all_to_all(blocks, "x", 0, 0, tiled=True)
    gram = gram_of(rows.reshape(-1, width), periods)
    own, gram = lax.optimization_barrier((field.reshape(-1, cells), gram))
    before = shift(own, 1)
    after = shift(own, -1)
    pieces = lax.all_to_all(gram.reshape(pairs, -1, 1, periods), PAIRS, 0, 0, tiled=True)
    copies = sum_and_copy(pieces, lax.axis_size("z"), LONG)
    pieces = lax.all_to_all(copies, "z", 0, 0, tiled=True)
    copies = sum_and_copy(pieces, groups * pairs, None)
    raw = lax.all_to_all(copies, ("x",) + PAIRS, 0, 0, tiled=True).reshape(-1, periods)
    before, after, _ = lax.optimization_barrier((before, after, copies))
    half = own.shape[0] // 2
    opposite = [shift(before[:half], 1), shift(after[half:], -1)]
    mix = refine(raw, gain, start_basis, lax.axis_index("x"), local, count)
    return project(mix, [own, after, *opposite, before]).reshape(field.shape)


def solution(mesh):
    cells, per = mesh.devices.shape
    split = Mesh(mesh.devices.reshape(4, cells // 8, 2, per), ("y", "z", "c", "x"))
    spec = P("x", None, None, ("y", "z", "c"))
    return jax.shard_map(
        per_device, mesh=split, in_specs=(spec, P(), P()), out_specs=spec, check_vma=False
    )
```

```python
import functools

import jax
import jax.numpy as jnp
from jax import lax
from jax.experimental import pallas as pl
from jax.experimental.pallas import tpu as pltpu
from jax.sharding import Mesh, PartitionSpec as P

ITERS = 3
PIVOTS = 4
LANES = 128
HIGH = lax.Precision.HIGHEST
PAIRS = ("y", "c")
VMEM = pl.BlockSpec(memory_space=pltpu.VMEM)
ANY = pl.BlockSpec(memory_space=pl.ANY)


def dot(a, b, ca, cb, precision=HIGH):
    return lax.dot_general(
        a, b, (((ca,), (cb,)), ((), ())), precision=precision, preferred_element_type=jnp.float32
    )


def halves(value):
    high = value.astype(jnp.bfloat16)
    return high, (value - high.astype(jnp.float32)).astype(jnp.bfloat16)


def tile_copies(block, held, first, sems, at):
    lanes = held.shape[1]
    tiles = block.shape[1] // lanes
    step = held.shape[0] // tiles
    return [
        pltpu.make_async_copy(
            block.at[:, pl.ds(c * lanes, lanes)],
            held.at[pl.ds(c * step + first, block.shape[0])],
            sems.at[at + c],
        )
        for c in range(tiles)
    ]


def lines(held, tiles, first, count, stride):
    step = held.shape[0] // tiles
    return jnp.concatenate(
        [held[pl.ds(c * step + first, count, stride=stride), :] for c in range(tiles)], axis=1
    )


def fold(acc, local, at):
    high = acc[:local, at : at + local] + acc[:local, at + local : at + 2 * local]
    low = acc[local:, at : at + local] + acc[local:, at + local : at + 2 * local]
    return high + low


def gram_kernel(local, group_ref, own_ref, before_ref, top_ref, bottom_ref, out_ref, *scratch):
    own, before, across, sems = scratch
    tiles = own_ref.shape[1] // LANES
    copies = tile_copies(own_ref, own, 0, sems, 0) + tile_copies(before_ref, before, 0, sems, tiles)
    copies += tile_copies(top_ref, across, 0, sems, 2 * tiles)
    copies += tile_copies(bottom_ref, across, top_ref.shape[0], sems, 3 * tiles)
    for copy in copies:
        copy.start()
    for copy in copies:
        copy.wait()
    per_period = own_ref.shape[0] // local
    half = per_period // 2
    second = group_ref[0] >= 2
    near, far = None, None
    for s in range(half):
        pair = [lines(own, tiles, s + t * half, local, per_period) for t in range(2)]
        for t in range(2):
            mine = halves(pair[t])
            other = halves(lines(before, tiles, s + t * half, local, per_period))
            part = dot(
                jnp.concatenate(mine, axis=0), jnp.concatenate(mine + other, axis=0), 1, 1, None
            )
            near = part if near is None else near + part
        mine = jnp.concatenate(halves(jnp.where(second, pair[1], pair[0])), axis=0)
        other = jnp.concatenate(halves(lines(across, tiles, s, local, half)), axis=0)
        part = dot(mine, other, 1, 1, None)
        far = part if far is None else far + part
    out_ref[...] = jnp.concatenate(
        [
            fold(near, local, 0),
            jnp.zeros((local, local), jnp.float32),
            fold(far, local, 0),
            fold(near, local, 2 * local),
        ],
        axis=1,
    )


def gram_of(group, own, before, top, bottom, local, periods):
    shape = (own.shape[0] * own.shape[1] // LANES, LANES)
    tiles = own.shape[1] // LANES
    return pl.pallas_call(
        functools.partial(gram_kernel, local),
        out_shape=jax.ShapeDtypeStruct((local, periods), jnp.float32),
        in_specs=[pl.BlockSpec(memory_space=pltpu.SMEM)] + [ANY] * 4,
        out_specs=VMEM,
        scratch_shapes=[
            pltpu.VMEM(shape, jnp.float32),
            pltpu.VMEM(shape, jnp.float32),
            pltpu.VMEM((shape[0] // 2, LANES), jnp.float32),
            pltpu.SemaphoreType.DMA((4 * tiles,)),
        ],
        compiler_params=pltpu.CompilerParams(vmem_limit_bytes=32 * 2**20),
        name="gram",
    )(group[None], own, before, top, bottom)


def assemble(parts, local):
    lane = lax.broadcasted_iota(jnp.int32, (local, parts.shape[1]), 1)
    slabs = []
    for at in range(0, parts.shape[0], local):
        slab = parts[at : at + local]
        slab = jnp.where(lane < local, 0.5 * slab, slab)
        slabs.append(pltpu.roll(slab, at, 1) if at else slab)
    half = jnp.concatenate(slabs, axis=0)
    return half + half.T


def inverse_factor(inner):
    rank = inner.shape[0]
    row = lax.broadcasted_iota(jnp.int32, (rank, rank), 0)
    col = lax.broadcasted_iota(jnp.int32, (rank, rank), 1)
    work = jnp.concatenate([inner, jnp.where(row == col, 1.0, 0.0)], axis=1)
    shape = work.shape
    sub = lax.broadcasted_iota(jnp.int32, shape, 0)
    pivots = jnp.ones(shape, jnp.float32)
    for start in range(0, rank, PIVOTS):
        ks = range(start, start + PIVOTS)
        columns = [jnp.broadcast_to(work[:, k : k + 1], shape) for k in ks]
        lines = [work[k : k + 1, :] for k in ks]
        for j, k in enumerate(ks):
            pivot = columns[j][k : k + 1, :]
            pivots = jnp.where(sub == k, pivot, pivots)
            factor = jnp.where(sub > k, columns[j] * (1.0 / pivot), 0.0)
            for i in range(j + 1, PIVOTS):
                columns[i] = columns[i] - factor * columns[i][k : k + 1, :]
                lines[i] = lines[i] - factor[start + i : start + i + 1, :] * lines[j]
            work = work - factor * lines[j]
    return work[:, rank:] * lax.rsqrt(pivots[:, rank:])


def project_kernel(count, local, group_ref, raw_ref, gain_ref, start_ref, *refs):
    own_ref, after_ref, before_ref, top_ref, bottom_ref, rest_ref = refs[:6]
    out_ref, held, across, ready, full_ref, in_sems, out_sems = refs[6:]
    height, cells = out_ref.shape
    tiles = cells // LANES
    group = group_ref[0]
    second = jnp.where(group >= 2, 1, 0)
    fetches = []
    for i, block in enumerate((own_ref, after_ref, before_ref)):
        fetches += tile_copies(block, held, i * height, in_sems, i * tiles)
    here, there = across.at[second], across.at[1 - second]
    fetches += tile_copies(top_ref, here, 0, in_sems, 3 * tiles)
    fetches += tile_copies(bottom_ref, here, top_ref.shape[0], in_sems, 4 * tiles)
    fetches += tile_copies(rest_ref, there, 0, in_sems, 5 * tiles)
    for fetch in fetches:
        fetch.start()
    gain = gain_ref[...]
    periods = gain.shape[1]
    per_period = height // local
    half = per_period // 2
    raw = assemble(raw_ref[...], local)

    def grow(basis):
        return dot(basis * gain, raw, 1, 0) * (gain * (1.0 / count))

    grown = grow(start_ref[...])
    for _ in range(ITERS - 1):
        later = grow(grown)
        grown = dot(inverse_factor(dot(grown, grown, 1, 1)), later, 1, 0)
    basis = dot(inverse_factor(dot(grown, grown, 1, 1)), grown, 1, 0)
    full_ref[...] = dot(basis, basis, 0, 0) * gain
    first = group * local
    own = full_ref[pl.ds(pl.multiple_of(first, local), local), :]
    high, low = halves(pltpu.roll(own, lax.rem(periods - first, periods), 1))
    mix = jnp.concatenate(
        [jnp.concatenate([high, high], axis=1), jnp.concatenate([low, jnp.zeros_like(low)], axis=1)],
        axis=0,
    )
    for fetch in fetches:
        fetch.wait()
    step = held.shape[0] // tiles
    side = across.shape[1] // tiles
    sends = []
    for pair in range(0, tiles, 2):
        for s in range(per_period):
            line = jnp.concatenate(
                [
                    jnp.concatenate(
                        [
                            held[pl.ds(c * step + s, 2 * local, stride=per_period), :],
                            across[s // half, pl.ds(c * side + s % half, local, stride=half), :],
                            held[
                                pl.ds(c * step + 2 * height + s, local, stride=per_period), :
                            ],
                        ],
                        axis=0,
                    )
                    for c in range(pair, pair + 2)
                ],
                axis=1,
            )
            result = dot(mix, jnp.concatenate(halves(line), axis=0), 1, 0, None)
            result = result[:local] + result[local:]
            for c in range(2):
                ready[pl.ds((pair + c) * height + s, local, stride=per_period), :] = result[
                    :, c * LANES : (c + 1) * LANES
                ]
        for c in range(pair, pair + 2):
            sends.append(
                pltpu.make_async_copy(
                    ready.at[pl.ds(c * height, height)],
                    out_ref.at[:, pl.ds(c * LANES, LANES)],
                    out_sems.at[c],
                )
            )
            sends[-1].start()
    for send in sends:
        send.wait()


def project(raw, gain, start_basis, group, blocks, local, count):
    height, cells = blocks[0].shape
    periods = gain.shape[0]
    tiles = cells // LANES
    return pl.pallas_call(
        functools.partial(project_kernel, count, local),
        out_shape=jax.ShapeDtypeStruct((height, cells), jnp.float32),
        in_specs=[pl.BlockSpec(memory_space=pltpu.SMEM)] + [VMEM] * 3 + [ANY] * len(blocks),
        out_specs=ANY,
        scratch_shapes=[
            pltpu.VMEM((tiles * 3 * height, LANES), jnp.float32),
            pltpu.VMEM((2, tiles * height // 2, LANES), jnp.float32),
            pltpu.VMEM((tiles * height, LANES), jnp.float32),
            pltpu.VMEM((periods, periods), jnp.float32),
            pltpu.SemaphoreType.DMA((len(blocks) * tiles,)),
            pltpu.SemaphoreType.DMA((tiles,)),
        ],
        compiler_params=pltpu.CompilerParams(vmem_limit_bytes=32 * 2**20),
        name="project",
    )(group[None], raw, gain[None, :], start_basis.T, *blocks)


def shift(value, step):
    count = lax.axis_size("x")
    return lax.ppermute(value, "x", [(i, (i + step) % count) for i in range(count)])


def copies_of(pieces, count):
    piece = jnp.sum(pieces, 0)
    return lax.optimization_barrier(jnp.broadcast_to(piece[None], (count,) + piece.shape))


def per_device(field, gain, start_basis):
    groups = lax.axis_size("x")
    group = lax.axis_index("x")
    local, parts, layers, cells = field.shape
    periods = gain.shape[0]
    pairs = lax.axis_size("y") * lax.axis_size("c")
    count = float(parts * layers * cells * lax.axis_size("z") * pairs)
    own = field.reshape(-1, cells)

    def side(block, part, first, size):
        block = block.reshape(field.shape)
        return lax.dynamic_slice(
            block, (first, part, 0, 0), (size, 1, layers, cells)
        ).reshape(-1, cells)

    sent = 1 - group // 2
    before = shift(own, 1)
    top = shift(shift(side(own, sent, 0, local // 2), -1), -1)
    bottom = shift(shift(side(own, sent, local // 2, local // 2), -1), -1)
    rest = shift(side(before, 1 - (group + 1) % groups // 2, 0, local), 1)
    source, top, bottom = lax.optimization_barrier((own, top, bottom))
    after = shift(source, -1)
    gram = gram_of(group, own, before, top, bottom, local, periods)
    pieces = lax.all_to_all(gram.reshape(pairs, -1, periods), PAIRS, 0, 0, tiled=True)
    copies, rest = lax.optimization_barrier((copies_of(pieces, lax.axis_size("z")), rest))
    pieces = lax.all_to_all(copies, "z", 0, 0, tiled=True)
    copies, after = lax.optimization_barrier((copies_of(pieces, groups * pairs), after))
    raw = lax.all_to_all(copies, ("x",) + PAIRS, 0, 0, tiled=True).reshape(periods, periods)
    blocks = [own, after, before, top, bottom, rest]
    result = project(raw, gain, start_basis, group, blocks, local, count)
    return result.reshape(field.shape)


def solution(mesh):
    cells, per = mesh.devices.shape
    split = Mesh(mesh.devices.reshape(4, cells // 8, 2, per), ("y", "z", "c", "x"))
    spec = P("x", None, None, ("y", "z", "c"))
    return jax.shard_map(
        per_device, mesh=split, in_specs=(spec, P(), P()), out_specs=spec, check_vma=False
    )
```

```python
import functools

import jax
import jax.numpy as jnp
from jax import lax
from jax.experimental import pallas as pl
from jax.experimental.pallas import tpu as pltpu
from jax.sharding import Mesh, PartitionSpec as P

ITERS = 3
PIVOTS = 4
LANES = 128
HIGH = lax.Precision.HIGHEST
PAIRS = ("y", "c")
VMEM = pl.BlockSpec(memory_space=pltpu.VMEM)
ANY = pl.BlockSpec(memory_space=pl.ANY)


def dot(a, b, ca, cb, precision=HIGH):
    return lax.dot_general(
        a, b, (((ca,), (cb,)), ((), ())), precision=precision, preferred_element_type=jnp.float32
    )


def halves(value):
    high = value.astype(jnp.bfloat16)
    return high, (value - high.astype(jnp.float32)).astype(jnp.bfloat16)


def tile_copies(block, held, first, sems, at):
    lanes = held.shape[1]
    tiles = block.shape[1] // lanes
    step = held.shape[0] // tiles
    return [
        pltpu.make_async_copy(
            block.at[:, pl.ds(c * lanes, lanes)],
            held.at[pl.ds(c * step + first, block.shape[0])],
            sems.at[at + c],
        )
        for c in range(tiles)
    ]


def lines(held, tiles, first, count, stride):
    step = held.shape[0] // tiles
    return jnp.concatenate(
        [held[pl.ds(c * step + first, count, stride=stride), :] for c in range(tiles)], axis=1
    )


def fold(acc, local, at):
    high = acc[:local, at : at + local] + acc[:local, at + local : at + 2 * local]
    low = acc[local:, at : at + local] + acc[local:, at + local : at + 2 * local]
    return high + low


def gram_kernel(local, group_ref, own_ref, before_ref, after_ref, out_ref, *scratch):
    own, before, after, sems = scratch
    tiles = own_ref.shape[1] // LANES
    copies = []
    for i, (block, held) in enumerate(((own_ref, own), (before_ref, before), (after_ref, after))):
        copies += tile_copies(block, held, 0, sems, i * tiles)
    for copy in copies:
        copy.start()
    for copy in copies:
        copy.wait()
    per_period = own_ref.shape[0] // local
    half = per_period // 2
    second = group_ref[0] >= 2
    near, far = None, None
    for s in range(half):
        left = [lines(before, tiles, s + t * half, local, per_period) for t in range(2)]
        for t in range(2):
            mine = halves(lines(own, tiles, s + t * half, local, per_period))
            both = jnp.concatenate(mine + halves(left[t]), axis=0)
            part = dot(jnp.concatenate(mine, axis=0), both, 1, 1, None)
            near = part if near is None else near + part
        right = jnp.concatenate(halves(lines(after, tiles, s, local, half)), axis=0)
        left = jnp.concatenate(halves(jnp.where(second, left[1], left[0])), axis=0)
        part = dot(left, right, 1, 1, None)
        far = part if far is None else far + part
    out_ref[...] = jnp.concatenate(
        [
            fold(near, local, 0),
            jnp.zeros((local, local), jnp.float32),
            fold(far, local, 0),
            fold(near, local, 2 * local),
        ],
        axis=1,
    )


def gram_of(group, own, before, after, local, periods):
    shape = (own.shape[0] * own.shape[1] // LANES, LANES)
    tiles = own.shape[1] // LANES
    return pl.pallas_call(
        functools.partial(gram_kernel, local),
        out_shape=jax.ShapeDtypeStruct((local, periods), jnp.float32),
        in_specs=[pl.BlockSpec(memory_space=pltpu.SMEM)] + [ANY] * 3,
        out_specs=VMEM,
        scratch_shapes=[
            pltpu.VMEM(shape, jnp.float32),
            pltpu.VMEM(shape, jnp.float32),
            pltpu.VMEM((shape[0] // 2, LANES), jnp.float32),
            pltpu.SemaphoreType.DMA((3 * tiles,)),
        ],
        compiler_params=pltpu.CompilerParams(vmem_limit_bytes=32 * 2**20),
        name="gram",
    )(group[None], own, before, after)


def assemble(parts, local):
    groups = parts.shape[0] // local
    lane = lax.broadcasted_iota(jnp.int32, (local, parts.shape[1]), 1)
    far = (lane >= 2 * local) & (lane < 3 * local)
    rows = [parts[g * local : (g + 1) * local] for g in range(groups)]
    slabs = []
    for g in range(groups):
        slab = jnp.where(far, rows[(g + 1) % groups], rows[g])
        slab = jnp.where(lane < local, 0.5 * slab, slab)
        slabs.append(pltpu.roll(slab, g * local, 1) if g else slab)
    half = jnp.concatenate(slabs, axis=0)
    return half + half.T


def inverse_factor(inner):
    rank = inner.shape[0]
    row = lax.broadcasted_iota(jnp.int32, (rank, rank), 0)
    col = lax.broadcasted_iota(jnp.int32, (rank, rank), 1)
    work = jnp.concatenate([inner, jnp.where(row == col, 1.0, 0.0)], axis=1)
    shape = work.shape
    sub = lax.broadcasted_iota(jnp.int32, shape, 0)
    pivots = jnp.ones(shape, jnp.float32)
    for start in range(0, rank, PIVOTS):
        ks = range(start, start + PIVOTS)
        columns = [jnp.broadcast_to(work[:, k : k + 1], shape) for k in ks]
        lines = [work[k : k + 1, :] for k in ks]
        for j, k in enumerate(ks):
            pivot = columns[j][k : k + 1, :]
            pivots = jnp.where(sub == k, pivot, pivots)
            factor = jnp.where(sub > k, columns[j] * (1.0 / pivot), 0.0)
            for i in range(j + 1, PIVOTS):
                columns[i] = columns[i] - factor * columns[i][k : k + 1, :]
                lines[i] = lines[i] - factor[start + i : start + i + 1, :] * lines[j]
            work = work - factor * lines[j]
    return work[:, rank:] * lax.rsqrt(pivots[:, rank:])


def project_kernel(count, local, group_ref, raw_ref, gain_ref, start_ref, *refs):
    own_ref, before_ref, *split_refs = refs[:6]
    out_ref, held, after, across, ready, full_ref, in_sems, out_sems = refs[6:]
    height, cells = out_ref.shape
    tiles = cells // LANES
    group = group_ref[0]
    second = jnp.where(group >= 2, 1, 0)
    later = jnp.where((group == 1) | (group == 2), 1, 0)
    fetches = tile_copies(own_ref, held, 0, in_sems, 0)
    fetches += tile_copies(before_ref, held, height, in_sems, tiles)
    places = (after.at[second], after.at[1 - second], across.at[later], across.at[1 - later])
    for i, (block, place) in enumerate(zip(split_refs, places)):
        fetches += tile_copies(block, place, 0, in_sems, (2 + i) * tiles)
    for fetch in fetches:
        fetch.start()
    gain = gain_ref[...]
    periods = gain.shape[1]
    per_period = height // local
    half = per_period // 2
    raw = assemble(raw_ref[...], local)

    def grow(basis):
        return dot(basis * gain, raw, 1, 0) * (gain * (1.0 / count))

    grown = grow(start_ref[...])
    for _ in range(ITERS - 1):
        later = grow(grown)
        grown = dot(inverse_factor(dot(grown, grown, 1, 1)), later, 1, 0)
    basis = dot(inverse_factor(dot(grown, grown, 1, 1)), grown, 1, 0)
    full_ref[...] = dot(basis, basis, 0, 0) * gain
    first = group * local
    own = full_ref[pl.ds(pl.multiple_of(first, local), local), :]
    high, low = halves(pltpu.roll(own, lax.rem(periods - first, periods), 1))
    mix = jnp.concatenate(
        [jnp.concatenate([high, high], axis=1), jnp.concatenate([low, jnp.zeros_like(low)], axis=1)],
        axis=0,
    )
    for fetch in fetches:
        fetch.wait()
    step = held.shape[0] // tiles
    side = across.shape[1] // tiles
    sends = []
    for pair in range(0, tiles, 2):
        for s in range(per_period):
            line = jnp.concatenate(
                [
                    jnp.concatenate(
                        [
                            held[pl.ds(c * step + s, local, stride=per_period), :],
                            after[s // half, pl.ds(c * side + s % half, local, stride=half), :],
                            across[s // half, pl.ds(c * side + s % half, local, stride=half), :],
                            held[pl.ds(c * step + height + s, local, stride=per_period), :],
                        ],
                        axis=0,
                    )
                    for c in range(pair, pair + 2)
                ],
                axis=1,
            )
            result = dot(mix, jnp.concatenate(halves(line), axis=0), 1, 0, None)
            result = result[:local] + result[local:]
            for c in range(2):
                ready[pl.ds((pair + c) * height + s, local, stride=per_period), :] = result[
                    :, c * LANES : (c + 1) * LANES
                ]
        for c in range(pair, pair + 2):
            sends.append(
                pltpu.make_async_copy(
                    ready.at[pl.ds(c * height, height)],
                    out_ref.at[:, pl.ds(c * LANES, LANES)],
                    out_sems.at[c],
                )
            )
            sends[-1].start()
    for send in sends:
        send.wait()


def project(raw, gain, start_basis, group, blocks, local, count):
    height, cells = blocks[0].shape
    periods = gain.shape[0]
    tiles = cells // LANES
    return pl.pallas_call(
        functools.partial(project_kernel, count, local),
        out_shape=jax.ShapeDtypeStruct((height, cells), jnp.float32),
        in_specs=[pl.BlockSpec(memory_space=pltpu.SMEM)] + [VMEM] * 3 + [ANY] * len(blocks),
        out_specs=ANY,
        scratch_shapes=[
            pltpu.VMEM((tiles * 2 * height, LANES), jnp.float32),
            pltpu.VMEM((2, tiles * height // 2, LANES), jnp.float32),
            pltpu.VMEM((2, tiles * height // 2, LANES), jnp.float32),
            pltpu.VMEM((tiles * height, LANES), jnp.float32),
            pltpu.VMEM((periods, periods), jnp.float32),
            pltpu.SemaphoreType.DMA((len(blocks) * tiles,)),
            pltpu.SemaphoreType.DMA((tiles,)),
        ],
        compiler_params=pltpu.CompilerParams(vmem_limit_bytes=32 * 2**20),
        name="project",
    )(group[None], raw, gain[None, :], start_basis.T, *blocks)


def shift(value, step):
    count = lax.axis_size("x")
    return lax.ppermute(value, "x", [(i, (i + step) % count) for i in range(count)])


def copies_of(pieces, count):
    piece = jnp.sum(pieces, 0)
    return lax.optimization_barrier(jnp.broadcast_to(piece[None], (count,) + piece.shape))


def per_device(field, gain, start_basis):
    groups = lax.axis_size("x")
    group = lax.axis_index("x")
    local, parts, layers, cells = field.shape
    periods = gain.shape[0]
    pairs = lax.axis_size("y") * lax.axis_size("c")
    count = float(parts * layers * cells * lax.axis_size("z") * pairs)
    own = field.reshape(-1, cells)

    def side(block, part):
        part = lax.dynamic_index_in_dim(block.reshape(field.shape), part, 1, keepdims=False)
        return part.reshape(-1, cells)

    sent = (group + groups - 1) % groups // 2
    before = shift(own, 1)
    after = shift(side(own, sent), -1)
    source, after = lax.optimization_barrier((own, after))
    rest = [shift(side(source, 1 - sent), -1), shift(after, -1)]
    gram = gram_of(group, own, before, after, local, periods)
    rest.append(shift(side(before, group // 2), 1))
    pieces = lax.all_to_all(gram.reshape(pairs, -1, periods), PAIRS, 0, 0, tiled=True)
    copies = copies_of(pieces, lax.axis_size("z"))
    pieces = lax.all_to_all(copies, "z", 0, 0, tiled=True)
    copies, rest = lax.optimization_barrier((copies_of(pieces, groups * pairs), rest))
    raw = lax.all_to_all(copies, ("x",) + PAIRS, 0, 0, tiled=True).reshape(periods, periods)
    blocks = [own, before, after, *rest]
    result = project(raw, gain, start_basis, group, blocks, local, count)
    return result.reshape(field.shape)


def solution(mesh):
    cells, per = mesh.devices.shape
    split = Mesh(mesh.devices.reshape(4, cells // 8, 2, per), ("y", "z", "c", "x"))
    spec = P("x", None, None, ("y", "z", "c"))
    return jax.shard_map(
        per_device, mesh=split, in_specs=(spec, P(), P()), out_specs=spec, check_vma=False
    )
```

```python
import functools

import jax
import jax.numpy as jnp
from jax import lax
from jax.experimental import pallas as pl
from jax.experimental.pallas import tpu as pltpu
from jax.sharding import Mesh, PartitionSpec as P

ITERS = 3
PIVOTS = 4
LANES = 128
HIGH = lax.Precision.HIGHEST
PAIRS = ("y", "c")
VMEM = pl.BlockSpec(memory_space=pltpu.VMEM)
ANY = pl.BlockSpec(memory_space=pl.ANY)


def dot(a, b, ca, cb, precision=HIGH):
    return lax.dot_general(
        a, b, (((ca,), (cb,)), ((), ())), precision=precision, preferred_element_type=jnp.float32
    )


def halves(value):
    high = value.astype(jnp.bfloat16)
    return high, (value - high.astype(jnp.float32)).astype(jnp.bfloat16)


def tile_copies(block, held, first, sems, at):
    lanes = held.shape[1]
    tiles = block.shape[1] // lanes
    step = held.shape[0] // tiles
    return [
        pltpu.make_async_copy(
            block.at[:, pl.ds(c * lanes, lanes)],
            held.at[pl.ds(c * step + first, block.shape[0])],
            sems.at[at + c],
        )
        for c in range(tiles)
    ]


def lines(held, tiles, first, count, stride):
    step = held.shape[0] // tiles
    return jnp.concatenate(
        [held[pl.ds(c * step + first, count, stride=stride), :] for c in range(tiles)], axis=1
    )


def fold(acc, local, at):
    high = acc[:local, at : at + local] + acc[:local, at + local : at + 2 * local]
    low = acc[local:, at : at + local] + acc[local:, at + local : at + 2 * local]
    return high + low


def gram_kernel(local, group_ref, own_ref, *refs):
    blocks, (out_ref, own, *held, sems) = refs[:3], refs[3:]
    tiles = own_ref.shape[1] // LANES
    copies = tile_copies(own_ref, own, 0, sems, 0)
    for i, block in enumerate(blocks):
        copies += tile_copies(block, held[i], 0, sems, (i + 1) * tiles)
    for copy in copies:
        copy.start()
    for copy in copies:
        copy.wait()
    per_period = own_ref.shape[0] // local
    half = per_period // 2
    second = group_ref[0] >= 2
    near, far = None, None
    for s in range(half):
        parts = [lines(own, tiles, s + t * half, local, per_period) for t in range(2)]
        parts = [jnp.where(second, parts[1 - t], parts[t]) for t in range(2)]
        first, other, after = (halves(lines(block, tiles, s, local, half)) for block in held)
        for part, before in zip(parts, (first, other)):
            mine = halves(part)
            both = jnp.concatenate(mine + before, axis=0)
            product = dot(jnp.concatenate(mine, axis=0), both, 1, 1, None)
            near = product if near is None else near + product
        product = dot(jnp.concatenate(first, axis=0), jnp.concatenate(after, axis=0), 1, 1, None)
        far = product if far is None else far + product
    out_ref[...] = jnp.concatenate(
        [
            fold(near, local, 0),
            jnp.zeros((local, local), jnp.float32),
            fold(far, local, 0),
            fold(near, local, 2 * local),
        ],
        axis=1,
    )


def gram_of(group, own, blocks, local, periods):
    shape = (own.shape[0] * own.shape[1] // LANES, LANES)
    tiles = own.shape[1] // LANES
    return pl.pallas_call(
        functools.partial(gram_kernel, local),
        out_shape=jax.ShapeDtypeStruct((local, periods), jnp.float32),
        in_specs=[pl.BlockSpec(memory_space=pltpu.SMEM)] + [ANY] * 4,
        out_specs=VMEM,
        scratch_shapes=[pltpu.VMEM(shape, jnp.float32)]
        + [pltpu.VMEM((shape[0] // 2, LANES), jnp.float32)] * 3
        + [pltpu.SemaphoreType.DMA((4 * tiles,))],
        compiler_params=pltpu.CompilerParams(vmem_limit_bytes=32 * 2**20),
        name="gram",
    )(group[None], own, *blocks)


def assemble(parts, local):
    groups = parts.shape[0] // local
    lane = lax.broadcasted_iota(jnp.int32, (local, parts.shape[1]), 1)
    far = (lane >= 2 * local) & (lane < 3 * local)
    rows = [parts[g * local : (g + 1) * local] for g in range(groups)]
    slabs = []
    for g in range(groups):
        slab = jnp.where(far, rows[(g + 1) % groups], rows[g])
        slab = jnp.where(lane < local, 0.5 * slab, slab)
        slabs.append(pltpu.roll(slab, g * local, 1) if g else slab)
    half = jnp.concatenate(slabs, axis=0)
    return half + half.T


def inverse_factor(inner):
    rank = inner.shape[0]
    row = lax.broadcasted_iota(jnp.int32, (rank, rank), 0)
    col = lax.broadcasted_iota(jnp.int32, (rank, rank), 1)
    work = jnp.concatenate([inner, jnp.where(row == col, 1.0, 0.0)], axis=1)
    shape = work.shape
    sub = lax.broadcasted_iota(jnp.int32, shape, 0)
    pivots = jnp.ones(shape, jnp.float32)
    for start in range(0, rank, PIVOTS):
        ks = range(start, start + PIVOTS)
        columns = [jnp.broadcast_to(work[:, k : k + 1], shape) for k in ks]
        lines = [work[k : k + 1, :] for k in ks]
        for j, k in enumerate(ks):
            pivot = columns[j][k : k + 1, :]
            pivots = jnp.where(sub == k, pivot, pivots)
            factor = jnp.where(sub > k, columns[j] * (1.0 / pivot), 0.0)
            for i in range(j + 1, PIVOTS):
                columns[i] = columns[i] - factor * columns[i][k : k + 1, :]
                lines[i] = lines[i] - factor[start + i : start + i + 1, :] * lines[j]
            work = work - factor * lines[j]
    return work[:, rank:] * lax.rsqrt(pivots[:, rank:])


def project_kernel(count, local, group_ref, raw_ref, start_ref, *refs):
    own_ref, *split_refs = refs[:7]
    out_ref, held, after, across, before, ready, full_ref, in_sems, out_sems = refs[7:]
    height, cells = out_ref.shape
    tiles = cells // LANES
    group = group_ref[0]
    second = jnp.where(group >= 2, 1, 0)
    later = jnp.where((group == 1) | (group == 2), 1, 0)
    fetches = tile_copies(own_ref, held, 0, in_sems, 0)
    ends = ((after, second), (across, later), (before, second))
    places = [place.at[end] for place, first in ends for end in (first, 1 - first)]
    for i, (block, place) in enumerate(zip(split_refs, places)):
        fetches += tile_copies(block, place, 0, in_sems, (1 + i) * tiles)
    for fetch in fetches:
        fetch.start()
    rank = start_ref.shape[0] - 1
    gain = start_ref[rank:]
    periods = gain.shape[1]
    per_period = height // local
    half = per_period // 2
    raw = assemble(raw_ref[...], local)

    def grow(basis):
        return dot(basis * gain, raw, 1, 0) * (gain * (1.0 / count))

    grown = grow(start_ref[:rank])
    for _ in range(ITERS - 1):
        later = grow(grown)
        grown = dot(inverse_factor(dot(grown, grown, 1, 1)), later, 1, 0)
    basis = dot(inverse_factor(dot(grown, grown, 1, 1)), grown, 1, 0)
    full_ref[...] = dot(basis, basis, 0, 0) * gain
    first = group * local
    own = full_ref[pl.ds(pl.multiple_of(first, local), local), :]
    high, low = halves(pltpu.roll(own, lax.rem(periods - first, periods), 1))
    mix = jnp.concatenate(
        [jnp.concatenate([high, high], axis=1), jnp.concatenate([low, jnp.zeros_like(low)], axis=1)],
        axis=0,
    )
    for fetch in fetches:
        fetch.wait()
    step = held.shape[0] // tiles
    side = across.shape[1] // tiles
    sends = []
    for pair in range(0, tiles, 2):
        for s in range(per_period):
            line = jnp.concatenate(
                [
                    jnp.concatenate(
                        [
                            held[pl.ds(c * step + s, local, stride=per_period), :],
                            *(
                                split[s // half, pl.ds(c * side + s % half, local, stride=half), :]
                                for split in (after, across, before)
                            ),
                        ],
                        axis=0,
                    )
                    for c in range(pair, pair + 2)
                ],
                axis=1,
            )
            result = dot(mix, jnp.concatenate(halves(line), axis=0), 1, 0, None)
            result = result[:local] + result[local:]
            for c in range(2):
                ready[pl.ds((pair + c) * height + s, local, stride=per_period), :] = result[
                    :, c * LANES : (c + 1) * LANES
                ]
        for c in range(pair, pair + 2):
            sends.append(
                pltpu.make_async_copy(
                    ready.at[pl.ds(c * height, height)],
                    out_ref.at[:, pl.ds(c * LANES, LANES)],
                    out_sems.at[c],
                )
            )
            sends[-1].start()
    for send in sends:
        send.wait()


def project(raw, start, group, blocks, local, count):
    height, cells = blocks[0].shape
    periods = start.shape[1]
    tiles = cells // LANES
    return pl.pallas_call(
        functools.partial(project_kernel, count, local),
        out_shape=jax.ShapeDtypeStruct((height, cells), jnp.float32),
        in_specs=[pl.BlockSpec(memory_space=pltpu.SMEM)] + [VMEM] * 2 + [ANY] * len(blocks),
        out_specs=ANY,
        scratch_shapes=[pltpu.VMEM((tiles * height, LANES), jnp.float32)]
        + [pltpu.VMEM((2, tiles * height // 2, LANES), jnp.float32)] * 3
        + [
            pltpu.VMEM((tiles * height, LANES), jnp.float32),
            pltpu.VMEM((periods, periods), jnp.float32),
            pltpu.SemaphoreType.DMA((len(blocks) * tiles,)),
            pltpu.SemaphoreType.DMA((tiles,)),
        ],
        compiler_params=pltpu.CompilerParams(vmem_limit_bytes=32 * 2**20),
        name="project",
    )(group[None], raw, start, *blocks)


def shift(value, step):
    count = lax.axis_size("x")
    return lax.ppermute(value, "x", [(i, (i + step) % count) for i in range(count)])


def copies_of(pieces, count):
    piece = jnp.sum(pieces, 0)
    return lax.optimization_barrier(jnp.broadcast_to(piece[None], (count,) + piece.shape))


def per_device(field, gain, start_basis):
    groups = lax.axis_size("x")
    group = lax.axis_index("x")
    local, parts, layers, cells = field.shape
    periods = gain.shape[0]
    pairs = lax.axis_size("y") * lax.axis_size("c")
    count = float(parts * layers * cells * lax.axis_size("z") * pairs)
    own = field.reshape(-1, cells)

    def side(block, part):
        part = lax.dynamic_index_in_dim(block.reshape(field.shape), part, 1, keepdims=False)
        return part.reshape(-1, cells)

    sent = (group + groups - 1) % groups // 2
    start = jnp.concatenate([start_basis.T, gain[None]], axis=0)
    one = side(own, 1 - sent)
    first = shift(one, 1)
    two = side(own, sent)
    after = shift(two, -1)
    second = shift(two, 1)
    first, start = lax.optimization_barrier((first, start))
    one, after, _ = lax.optimization_barrier((one, after, first))
    rest = [shift(one, -1), shift(after, -1), shift(first, 1)]
    gram = gram_of(group, own, [first, second, after], local, periods)
    pieces = lax.all_to_all(gram.reshape(pairs, -1, periods), PAIRS, 0, 0, tiled=True)
    copies = copies_of(pieces, lax.axis_size("z"))
    pieces = lax.all_to_all(copies, "z", 0, 0, tiled=True)
    copies, rest = lax.optimization_barrier((copies_of(pieces, groups * pairs), rest))
    raw = lax.all_to_all(copies, ("x",) + PAIRS, 0, 0, tiled=True).reshape(periods, periods)
    blocks = [own, after, *rest, first, second]
    result = project(raw, start, group, blocks, local, count)
    return result.reshape(field.shape)


def solution(mesh):
    cells, per = mesh.devices.shape
    split = Mesh(mesh.devices.reshape(4, cells // 8, 2, per), ("y", "z", "c", "x"))
    spec = P("x", None, None, ("y", "z", "c"))
    return jax.shard_map(
        per_device, mesh=split, in_specs=(spec, P(), P()), out_specs=spec, check_vma=False
    )
```

```python
import functools

import jax
import jax.numpy as jnp
from jax import lax
from jax.experimental import pallas as pl
from jax.experimental.pallas import tpu as pltpu
from jax.sharding import Mesh, PartitionSpec as P

ITERS = 3
PIVOTS = 16
LANES = 128
HIGH = lax.Precision.HIGHEST
PAIRS = ("y", "c")
VMEM = pl.BlockSpec(memory_space=pltpu.VMEM)
ANY = pl.BlockSpec(memory_space=pl.ANY)


def dot(a, b, ca, cb, precision=HIGH):
    return lax.dot_general(
        a, b, (((ca,), (cb,)), ((), ())), precision=precision, preferred_element_type=jnp.float32
    )


def halves(value):
    high = value.astype(jnp.bfloat16)
    return high, (value - high.astype(jnp.float32)).astype(jnp.bfloat16)


def tile_copies(block, held, first, sems, at):
    lanes = held.shape[1]
    tiles = block.shape[1] // lanes
    step = held.shape[0] // tiles
    return [
        pltpu.make_async_copy(
            block.at[:, pl.ds(c * lanes, lanes)],
            held.at[pl.ds(c * step + first, block.shape[0])],
            sems.at[at + c],
        )
        for c in range(tiles)
    ]


def lines(held, tiles, first, count, stride):
    step = held.shape[0] // tiles
    return jnp.concatenate(
        [held[pl.ds(c * step + first, count, stride=stride), :] for c in range(tiles)], axis=1
    )


def fold(acc, local, at):
    high = acc[:local, at : at + local] + acc[:local, at + local : at + 2 * local]
    low = acc[local:, at : at + local] + acc[local:, at + local : at + 2 * local]
    return high + low


def gram_kernel(local, group_ref, own_ref, *refs):
    blocks, (out_ref, own, *held, sems) = refs[:3], refs[3:]
    tiles = own_ref.shape[1] // LANES
    copies = tile_copies(own_ref, own, 0, sems, 0)
    for i, block in enumerate(blocks):
        copies += tile_copies(block, held[i], 0, sems, (i + 1) * tiles)
    for copy in copies:
        copy.start()
    for copy in copies:
        copy.wait()
    per_period = own_ref.shape[0] // local
    half = per_period // 2
    second = group_ref[0] >= 2
    near, far = None, None
    for s in range(half):
        parts = [lines(own, tiles, s + t * half, local, per_period) for t in range(2)]
        parts = [jnp.where(second, parts[1 - t], parts[t]) for t in range(2)]
        first, other, after = (halves(lines(block, tiles, s, local, half)) for block in held)
        for part, before in zip(parts, (first, other)):
            mine = halves(part)
            both = jnp.concatenate(mine + before, axis=0)
            product = dot(jnp.concatenate(mine, axis=0), both, 1, 1, None)
            near = product if near is None else near + product
        product = dot(jnp.concatenate(first, axis=0), jnp.concatenate(after, axis=0), 1, 1, None)
        far = product if far is None else far + product
    out_ref[...] = jnp.concatenate(
        [
            fold(near, local, 0),
            jnp.zeros((local, local), jnp.float32),
            fold(far, local, 0),
            fold(near, local, 2 * local),
        ],
        axis=1,
    )


def gram_of(group, own, blocks, local, periods):
    shape = (own.shape[0] * own.shape[1] // LANES, LANES)
    tiles = own.shape[1] // LANES
    return pl.pallas_call(
        functools.partial(gram_kernel, local),
        out_shape=jax.ShapeDtypeStruct((local, periods), jnp.float32),
        in_specs=[pl.BlockSpec(memory_space=pltpu.SMEM)] + [ANY] * 4,
        out_specs=VMEM,
        scratch_shapes=[pltpu.VMEM(shape, jnp.float32)]
        + [pltpu.VMEM((shape[0] // 2, LANES), jnp.float32)] * 3
        + [pltpu.SemaphoreType.DMA((4 * tiles,))],
        compiler_params=pltpu.CompilerParams(vmem_limit_bytes=32 * 2**20),
        name="gram",
    )(group[None], own, *blocks)


def assemble(parts, local):
    groups = parts.shape[0] // local
    lane = lax.broadcasted_iota(jnp.int32, (local, parts.shape[1]), 1)
    far = (lane >= 2 * local) & (lane < 3 * local)
    rows = [parts[g * local : (g + 1) * local] for g in range(groups)]
    slabs = []
    for g in range(groups):
        slab = jnp.where(far, rows[(g + 1) % groups], rows[g])
        slab = jnp.where(lane < local, 0.5 * slab, slab)
        slabs.append(pltpu.roll(slab, g * local, 1) if g else slab)
    half = jnp.concatenate(slabs, axis=0)
    return half + half.T


def inverse_factor(inner):
    rank = inner.shape[0]
    row = lax.broadcasted_iota(jnp.int32, (rank, rank), 0)
    col = lax.broadcasted_iota(jnp.int32, (rank, rank), 1)
    work = jnp.concatenate([inner, jnp.where(row == col, 1.0, 0.0)], axis=1)
    shape = work.shape
    sub = lax.broadcasted_iota(jnp.int32, shape, 0)
    pivots = jnp.ones(shape, jnp.float32)
    for start in range(0, rank, PIVOTS):
        ks = range(start, start + PIVOTS)
        columns = [jnp.broadcast_to(work[:, k : k + 1], shape) for k in ks]
        lines = [work[k : k + 1, :] for k in ks]
        for j, k in enumerate(ks):
            pivot = columns[j][k : k + 1, :]
            pivots = jnp.where(sub == k, pivot, pivots)
            factor = jnp.where(sub > k, columns[j] * (1.0 / pivot), 0.0)
            for i in range(j + 1, PIVOTS):
                columns[i] = columns[i] - factor * columns[i][k : k + 1, :]
                lines[i] = lines[i] - factor[start + i : start + i + 1, :] * lines[j]
            work = work - factor * lines[j]
    return work[:, rank:] * lax.rsqrt(pivots[:, rank:])


def project_kernel(count, local, group_ref, raw_ref, start_ref, *refs):
    own_ref, *split_refs = refs[:7]
    out_ref, held, after, across, before, ready, full_ref, in_sems, out_sems = refs[7:]
    height, cells = out_ref.shape
    tiles = cells // LANES
    group = group_ref[0]
    second = jnp.where(group >= 2, 1, 0)
    later = jnp.where((group == 1) | (group == 2), 1, 0)
    fetches = tile_copies(own_ref, held, 0, in_sems, 0)
    ends = ((after, second), (across, later), (before, second))
    places = [place.at[end] for place, first in ends for end in (first, 1 - first)]
    for i, (block, place) in enumerate(zip(split_refs, places)):
        fetches += tile_copies(block, place, 0, in_sems, (1 + i) * tiles)
    for fetch in fetches:
        fetch.start()
    rank = start_ref.shape[0] - 1
    gain = start_ref[rank:]
    periods = gain.shape[1]
    per_period = height // local
    half = per_period // 2
    raw = assemble(raw_ref[...], local)

    def grow(basis):
        return dot(basis * gain, raw, 1, 0) * (gain * (1.0 / count))

    grown = grow(start_ref[:rank])
    for _ in range(ITERS - 1):
        later = grow(grown)
        grown = dot(inverse_factor(dot(grown, grown, 1, 1)), later, 1, 0)
    basis = dot(inverse_factor(dot(grown, grown, 1, 1)), grown, 1, 0)
    full_ref[...] = dot(basis, basis, 0, 0) * gain
    first = group * local
    own = full_ref[pl.ds(pl.multiple_of(first, local), local), :]
    high, low = halves(pltpu.roll(own, lax.rem(periods - first, periods), 1))
    mix = jnp.concatenate(
        [jnp.concatenate([high, high], axis=1), jnp.concatenate([low, jnp.zeros_like(low)], axis=1)],
        axis=0,
    )
    for fetch in fetches:
        fetch.wait()
    step = held.shape[0] // tiles
    side = across.shape[1] // tiles
    sends = []
    for pair in range(0, tiles, 2):
        for s in range(per_period):
            line = jnp.concatenate(
                [
                    jnp.concatenate(
                        [
                            held[pl.ds(c * step + s, local, stride=per_period), :],
                            *(
                                split[s // half, pl.ds(c * side + s % half, local, stride=half), :]
                                for split in (after, across, before)
                            ),
                        ],
                        axis=0,
                    )
                    for c in range(pair, pair + 2)
                ],
                axis=1,
            )
            result = dot(mix, jnp.concatenate(halves(line), axis=0), 1, 0, None)
            result = result[:local] + result[local:]
            for c in range(2):
                ready[pl.ds((pair + c) * height + s, local, stride=per_period), :] = result[
                    :, c * LANES : (c + 1) * LANES
                ]
        for c in range(pair, pair + 2):
            sends.append(
                pltpu.make_async_copy(
                    ready.at[pl.ds(c * height, height)],
                    out_ref.at[:, pl.ds(c * LANES, LANES)],
                    out_sems.at[c],
                )
            )
            sends[-1].start()
    for send in sends:
        send.wait()


def project(raw, start, group, blocks, local, count):
    height, cells = blocks[0].shape
    periods = start.shape[1]
    tiles = cells // LANES
    return pl.pallas_call(
        functools.partial(project_kernel, count, local),
        out_shape=jax.ShapeDtypeStruct((height, cells), jnp.float32),
        in_specs=[pl.BlockSpec(memory_space=pltpu.SMEM)] + [VMEM] * 2 + [ANY] * len(blocks),
        out_specs=ANY,
        scratch_shapes=[pltpu.VMEM((tiles * height, LANES), jnp.float32)]
        + [pltpu.VMEM((2, tiles * height // 2, LANES), jnp.float32)] * 3
        + [
            pltpu.VMEM((tiles * height, LANES), jnp.float32),
            pltpu.VMEM((periods, periods), jnp.float32),
            pltpu.SemaphoreType.DMA((len(blocks) * tiles,)),
            pltpu.SemaphoreType.DMA((tiles,)),
        ],
        compiler_params=pltpu.CompilerParams(vmem_limit_bytes=32 * 2**20),
        name="project",
    )(group[None], raw, start, *blocks)


def shift(value, step):
    count = lax.axis_size("x")
    return lax.ppermute(value, "x", [(i, (i + step) % count) for i in range(count)])


def copies_of(pieces, count):
    piece = jnp.sum(pieces, 0)
    return lax.optimization_barrier(jnp.broadcast_to(piece[None], (count,) + piece.shape))


def per_device(field, gain, start_basis):
    groups = lax.axis_size("x")
    group = lax.axis_index("x")
    local, parts, layers, cells = field.shape
    periods = gain.shape[0]
    pairs = lax.axis_size("y") * lax.axis_size("c")
    count = float(parts * layers * cells * lax.axis_size("z") * pairs)
    own = field.reshape(-1, cells)

    def side(block, part):
        part = lax.dynamic_index_in_dim(block.reshape(field.shape), part, 1, keepdims=False)
        return part.reshape(-1, cells)

    sent = (group + groups - 1) % groups // 2
    start = jnp.concatenate([start_basis.T, gain[None]], axis=0)
    one = side(own, 1 - sent)
    source, one = lax.optimization_barrier((own, one))
    first = shift(one, 1)
    two = side(source, sent)
    after = shift(two, -1)
    second = shift(two, 1)
    first, start = lax.optimization_barrier((first, start))
    one, after, _ = lax.optimization_barrier((one, after, first))
    rest = [shift(one, -1), shift(after, -1), shift(first, 1)]
    gram = gram_of(group, own, [first, second, after], local, periods)
    pieces = lax.all_to_all(gram.reshape(pairs, -1, periods), PAIRS, 0, 0, tiled=True)
    copies = copies_of(pieces, lax.axis_size("z"))
    pieces = lax.all_to_all(copies, "z", 0, 0, tiled=True)
    copies, rest = lax.optimization_barrier((copies_of(pieces, groups * pairs), rest))
    raw = lax.all_to_all(copies, ("x",) + PAIRS, 0, 0, tiled=True).reshape(periods, periods)
    blocks = [own, after, *rest, first, second]
    result = project(raw, start, group, blocks, local, count)
    return result.reshape(field.shape)


def solution(mesh):
    cells, per = mesh.devices.shape
    split = Mesh(mesh.devices.reshape(4, cells // 8, 2, per), ("y", "z", "c", "x"))
    spec = P("x", None, None, ("y", "z", "c"))
    return jax.shard_map(
        per_device, mesh=split, in_specs=(spec, P(), P()), out_specs=spec, check_vma=False
    )
```

```python
import functools

import jax
import jax.numpy as jnp
from jax import lax
from jax.experimental import pallas as pl
from jax.experimental.pallas import tpu as pltpu
from jax.sharding import Mesh, PartitionSpec as P

ITERS = 3
PIVOTS = 16
LANES = 128
HIGH = lax.Precision.HIGHEST
PAIRS = ("y", "c")
VMEM = pl.BlockSpec(memory_space=pltpu.VMEM)
ANY = pl.BlockSpec(memory_space=pl.ANY)


def dot(a, b, ca, cb, precision=HIGH):
    return lax.dot_general(
        a, b, (((ca,), (cb,)), ((), ())), precision=precision, preferred_element_type=jnp.float32
    )


def halves(value):
    high = value.astype(jnp.bfloat16)
    return high, (value - high.astype(jnp.float32)).astype(jnp.bfloat16)


def tile_copies(block, held, first, sems, at):
    lanes = held.shape[1]
    tiles = block.shape[1] // lanes
    step = held.shape[0] // tiles
    return [
        pltpu.make_async_copy(
            block.at[:, pl.ds(c * lanes, lanes)],
            held.at[pl.ds(c * step + first, block.shape[0])],
            sems.at[at + c],
        )
        for c in range(tiles)
    ]


def lines(held, tiles, first, count, stride):
    step = held.shape[0] // tiles
    return jnp.concatenate(
        [held[pl.ds(c * step + first, count, stride=stride), :] for c in range(tiles)], axis=1
    )


def fold(acc, local, at):
    high = acc[:local, at : at + local] + acc[:local, at + local : at + 2 * local]
    low = acc[local:, at : at + local] + acc[local:, at + local : at + 2 * local]
    return high + low


def gram_kernel(local, group_ref, own_ref, *refs):
    blocks, (out_ref, own, *held, sems) = refs[:3], refs[3:]
    tiles = own_ref.shape[1] // LANES
    copies = tile_copies(own_ref, own, 0, sems, 0)
    for i, block in enumerate(blocks):
        copies += tile_copies(block, held[i], 0, sems, (i + 1) * tiles)
    for copy in copies:
        copy.start()
    for copy in copies:
        copy.wait()
    per_period = own_ref.shape[0] // local
    half = per_period // 2
    second = group_ref[0] >= 2
    near, far = None, None
    for s in range(half):
        parts = [lines(own, tiles, s + t * half, local, per_period) for t in range(2)]
        parts = [jnp.where(second, parts[1 - t], parts[t]) for t in range(2)]
        first, other, after = (halves(lines(block, tiles, s, local, half)) for block in held)
        for part, before in zip(parts, (first, other)):
            mine = halves(part)
            both = jnp.concatenate(mine + before, axis=0)
            product = dot(jnp.concatenate(mine, axis=0), both, 1, 1, None)
            near = product if near is None else near + product
        product = dot(jnp.concatenate(first, axis=0), jnp.concatenate(after, axis=0), 1, 1, None)
        far = product if far is None else far + product
    out_ref[...] = jnp.concatenate(
        [
            fold(near, local, 0),
            jnp.zeros((local, local), jnp.float32),
            fold(far, local, 0),
            fold(near, local, 2 * local),
        ],
        axis=1,
    )


def gram_of(group, own, blocks, local, periods):
    shape = (own.shape[0] * own.shape[1] // LANES, LANES)
    tiles = own.shape[1] // LANES
    return pl.pallas_call(
        functools.partial(gram_kernel, local),
        out_shape=jax.ShapeDtypeStruct((local, periods), jnp.float32),
        in_specs=[pl.BlockSpec(memory_space=pltpu.SMEM)] + [ANY] * 4,
        out_specs=VMEM,
        scratch_shapes=[pltpu.VMEM(shape, jnp.float32)]
        + [pltpu.VMEM((shape[0] // 2, LANES), jnp.float32)] * 3
        + [pltpu.SemaphoreType.DMA((4 * tiles,))],
        compiler_params=pltpu.CompilerParams(vmem_limit_bytes=32 * 2**20),
        name="gram",
    )(group[None], own, *blocks)


def assemble(rows):
    groups = len(rows)
    local = rows[0].shape[0]
    lane = lax.broadcasted_iota(jnp.int32, rows[0].shape, 1)
    far = (lane >= 2 * local) & (lane < 3 * local)
    slabs = []
    for g in range(groups):
        slab = jnp.where(far, rows[(g + 1) % groups], rows[g])
        slab = jnp.where(lane < local, 0.5 * slab, slab)
        slabs.append(pltpu.roll(slab, g * local, 1) if g else slab)
    half = jnp.concatenate(slabs, axis=0)
    return half + half.T


def inverse_factor(inner):
    rank = inner.shape[0]
    row = lax.broadcasted_iota(jnp.int32, (rank, rank), 0)
    col = lax.broadcasted_iota(jnp.int32, (rank, rank), 1)
    work = jnp.concatenate([inner, jnp.where(row == col, 1.0, 0.0)], axis=1)
    shape = work.shape
    sub = lax.broadcasted_iota(jnp.int32, shape, 0)
    pivots = jnp.ones(shape, jnp.float32)
    for start in range(0, rank, PIVOTS):
        ks = range(start, start + PIVOTS)
        columns = [jnp.broadcast_to(work[:, k : k + 1], shape) for k in ks]
        lines = [work[k : k + 1, :] for k in ks]
        for j, k in enumerate(ks):
            pivot = columns[j][k : k + 1, :]
            pivots = jnp.where(sub == k, pivot, pivots)
            factor = jnp.where(sub > k, columns[j] * (1.0 / pivot), 0.0)
            for i in range(j + 1, PIVOTS):
                columns[i] = columns[i] - factor * columns[i][k : k + 1, :]
                lines[i] = lines[i] - factor[start + i : start + i + 1, :] * lines[j]
            work = work - factor * lines[j]
    return work[:, rank:] * lax.rsqrt(pivots[:, rank:])


def project_kernel(count, local, group_ref, raw_ref, start_ref, *refs):
    own_ref, *split_refs = refs[:7]
    out_ref, held, after, across, before, ready, in_sems, out_sems = refs[7:]
    height, cells = out_ref.shape
    tiles = cells // LANES
    group = group_ref[0]
    second = jnp.where(group >= 2, 1, 0)
    later = jnp.where((group == 1) | (group == 2), 1, 0)
    fetches = tile_copies(own_ref, held, 0, in_sems, 0)
    ends = ((after, second), (across, later), (before, second))
    places = [place.at[end] for place, first in ends for end in (first, 1 - first)]
    for i, (block, place) in enumerate(zip(split_refs, places)):
        fetches += tile_copies(block, place, 0, in_sems, (1 + i) * tiles)
    for fetch in fetches:
        fetch.start()
    rank = start_ref.shape[0] - 1
    periods = start_ref.shape[1]
    groups = periods // local
    start = pltpu.roll(start_ref[...], lax.rem(periods - group * local, periods), 1)
    gain = start[rank:]
    per_period = height // local
    half = per_period // 2
    firsts = [pl.multiple_of(lax.rem(group + g, groups) * local, local) for g in range(groups)]
    raw = assemble([raw_ref[pl.ds(first, local), :] for first in firsts])

    def grow(basis):
        return dot(basis * gain, raw, 1, 0) * (gain * (1.0 / count))

    grown = grow(start[:rank])
    for _ in range(ITERS - 1):
        later = grow(grown)
        grown = dot(inverse_factor(dot(grown, grown, 1, 1)), later, 1, 0)
    basis = dot(inverse_factor(dot(grown, grown, 1, 1)), grown, 1, 0)
    high, low = halves(dot(basis[:, :local], basis * gain, 0, 0))
    mix = jnp.concatenate(
        [jnp.concatenate([high, high], axis=1), jnp.concatenate([low, jnp.zeros_like(low)], axis=1)],
        axis=0,
    )
    for fetch in fetches:
        fetch.wait()
    step = held.shape[0] // tiles
    side = across.shape[1] // tiles
    sends = []
    for pair in range(0, tiles, 2):
        for s in range(per_period):
            line = jnp.concatenate(
                [
                    jnp.concatenate(
                        [
                            held[pl.ds(c * step + s, local, stride=per_period), :],
                            *(
                                split[s // half, pl.ds(c * side + s % half, local, stride=half), :]
                                for split in (after, across, before)
                            ),
                        ],
                        axis=0,
                    )
                    for c in range(pair, pair + 2)
                ],
                axis=1,
            )
            result = dot(mix, jnp.concatenate(halves(line), axis=0), 1, 0, None)
            result = result[:local] + result[local:]
            for c in range(2):
                ready[pl.ds((pair + c) * height + s, local, stride=per_period), :] = result[
                    :, c * LANES : (c + 1) * LANES
                ]
        for c in range(pair, pair + 2):
            sends.append(
                pltpu.make_async_copy(
                    ready.at[pl.ds(c * height, height)],
                    out_ref.at[:, pl.ds(c * LANES, LANES)],
                    out_sems.at[c],
                )
            )
            sends[-1].start()
    for send in sends:
        send.wait()


def project(raw, start, group, blocks, local, count):
    height, cells = blocks[0].shape
    periods = start.shape[1]
    tiles = cells // LANES
    return pl.pallas_call(
        functools.partial(project_kernel, count, local),
        out_shape=jax.ShapeDtypeStruct((height, cells), jnp.float32),
        in_specs=[pl.BlockSpec(memory_space=pltpu.SMEM)] + [VMEM] * 2 + [ANY] * len(blocks),
        out_specs=ANY,
        scratch_shapes=[pltpu.VMEM((tiles * height, LANES), jnp.float32)]
        + [pltpu.VMEM((2, tiles * height // 2, LANES), jnp.float32)] * 3
        + [
            pltpu.VMEM((tiles * height, LANES), jnp.float32),
            pltpu.SemaphoreType.DMA((len(blocks) * tiles,)),
            pltpu.SemaphoreType.DMA((tiles,)),
        ],
        compiler_params=pltpu.CompilerParams(vmem_limit_bytes=32 * 2**20),
        name="project",
    )(group[None], raw, start, *blocks)


def shift(value, step):
    count = lax.axis_size("x")
    return lax.ppermute(value, "x", [(i, (i + step) % count) for i in range(count)])


def copies_of(pieces, count):
    piece = jnp.sum(pieces, 0)
    return lax.optimization_barrier(jnp.broadcast_to(piece[None], (count,) + piece.shape))


def per_device(field, gain, start_basis):
    groups = lax.axis_size("x")
    group = lax.axis_index("x")
    local, parts, layers, cells = field.shape
    periods = gain.shape[0]
    pairs = lax.axis_size("y") * lax.axis_size("c")
    count = float(parts * layers * cells * lax.axis_size("z") * pairs)
    own = field.reshape(-1, cells)

    def side(block, part):
        part = lax.dynamic_index_in_dim(block.reshape(field.shape), part, 1, keepdims=False)
        return part.reshape(-1, cells)

    sent = (group + groups - 1) % groups // 2
    start = jnp.concatenate([start_basis.T, gain[None]], axis=0)
    one = side(own, 1 - sent)
    source, one = lax.optimization_barrier((own, one))
    first = shift(one, 1)
    two = side(source, sent)
    after = shift(two, -1)
    second = shift(two, 1)
    first, start = lax.optimization_barrier((first, start))
    one, after, _ = lax.optimization_barrier((one, after, first))
    rest = [shift(one, -1), shift(after, -1), shift(first, 1)]
    gram = gram_of(group, own, [first, second, after], local, periods)
    pieces = lax.all_to_all(gram.reshape(pairs, -1, periods), PAIRS, 0, 0, tiled=True)
    copies = copies_of(pieces, lax.axis_size("z"))
    pieces = lax.all_to_all(copies, "z", 0, 0, tiled=True)
    copies, rest = lax.optimization_barrier((copies_of(pieces, groups * pairs), rest))
    raw = lax.all_to_all(copies, ("x",) + PAIRS, 0, 0, tiled=True).reshape(periods, periods)
    blocks = [own, after, *rest, first, second]
    result = project(raw, start, group, blocks, local, count)
    return result.reshape(field.shape)


def solution(mesh):
    cells, per = mesh.devices.shape
    split = Mesh(mesh.devices.reshape(4, cells // 8, 2, per), ("y", "z", "c", "x"))
    spec = P("x", None, None, ("y", "z", "c"))
    return jax.shard_map(
        per_device, mesh=split, in_specs=(spec, P(), P()), out_specs=spec, check_vma=False
    )
```

```python
import functools

import jax
import jax.numpy as jnp
from jax import lax
from jax.experimental import pallas as pl
from jax.experimental.pallas import tpu as pltpu
from jax.sharding import Mesh, PartitionSpec as P

ITERS = 3
PIVOTS = 16
LANES = 128
HIGH = lax.Precision.HIGHEST
PAIRS = ("y", "c")
VMEM = pl.BlockSpec(memory_space=pltpu.VMEM)
ANY = pl.BlockSpec(memory_space=pl.ANY)


def dot(a, b, ca, cb, precision=HIGH):
    return lax.dot_general(
        a, b, (((ca,), (cb,)), ((), ())), precision=precision, preferred_element_type=jnp.float32
    )


def halves(value):
    high = value.astype(jnp.bfloat16)
    return high, (value - high.astype(jnp.float32)).astype(jnp.bfloat16)


def tile_copies(block, held, first, sems, at):
    lanes = held.shape[1]
    tiles = block.shape[1] // lanes
    step = held.shape[0] // tiles
    return [
        pltpu.make_async_copy(
            block.at[:, pl.ds(c * lanes, lanes)],
            held.at[pl.ds(c * step + first, block.shape[0])],
            sems.at[at + c],
        )
        for c in range(tiles)
    ]


def lines(held, tiles, first, count, stride):
    step = held.shape[0] // tiles
    return jnp.concatenate(
        [held[pl.ds(c * step + first, count, stride=stride), :] for c in range(tiles)], axis=1
    )


def fold(acc, local, at):
    high = acc[:local, at : at + local] + acc[:local, at + local : at + 2 * local]
    low = acc[local:, at : at + local] + acc[local:, at + local : at + 2 * local]
    return high + low


def gram_kernel(local, place_ref, own_ref, *refs):
    blocks, (out_ref, own, *held, sems) = refs[:3], refs[3:]
    tiles = own_ref.shape[1] // LANES
    copies = tile_copies(own_ref, own, 0, sems, 0)
    for i, block in enumerate(blocks):
        copies += tile_copies(block, held[i], 0, sems, (i + 1) * tiles)
    for copy in copies:
        copy.start()
    for copy in copies:
        copy.wait()
    per_period = own_ref.shape[0] // local
    half = per_period // 2
    second = place_ref[1] >= 2
    mirrored = place_ref[2] > 0
    near, far = None, None
    for s in range(half):
        parts = [lines(own, tiles, s + t * half, local, per_period) for t in range(2)]
        parts = [jnp.where(second, parts[1 - t], parts[t]) for t in range(2)]
        first, other, after = (halves(lines(block, tiles, s, local, half)) for block in held)
        for part, before in zip(parts, (first, other)):
            mine = halves(part)
            both = jnp.concatenate(mine + before, axis=0)
            product = dot(jnp.concatenate(mine, axis=0), both, 1, 1, None)
            near = product if near is None else near + product
        product = dot(jnp.concatenate(first, axis=0), jnp.concatenate(after, axis=0), 1, 1, None)
        far = product if far is None else far + product
    far = fold(far, local, 0)
    side = fold(near, local, 2 * local)
    out_ref[...] = jnp.concatenate(
        [
            fold(near, local, 0),
            jnp.where(mirrored, side, 0.0),
            jnp.where(mirrored, far.T, far),
            jnp.where(mirrored, 0.0, side),
        ],
        axis=1,
    )


def gram_of(place, own, blocks, local, periods):
    shape = (own.shape[0] * own.shape[1] // LANES, LANES)
    tiles = own.shape[1] // LANES
    return pl.pallas_call(
        functools.partial(gram_kernel, local),
        out_shape=jax.ShapeDtypeStruct((local, periods), jnp.float32),
        in_specs=[pl.BlockSpec(memory_space=pltpu.SMEM)] + [ANY] * 4,
        out_specs=VMEM,
        scratch_shapes=[pltpu.VMEM(shape, jnp.float32)]
        + [pltpu.VMEM((shape[0] // 2, LANES), jnp.float32)] * 3
        + [pltpu.SemaphoreType.DMA((4 * tiles,))],
        compiler_params=pltpu.CompilerParams(vmem_limit_bytes=32 * 2**20),
        name="gram",
    )(place, own, *blocks)


def assemble(rows):
    groups = len(rows)
    local = rows[0].shape[0]
    lane = lax.broadcasted_iota(jnp.int32, rows[0].shape, 1)
    far = (lane >= 2 * local) & (lane < 3 * local)
    slabs = []
    for g in range(groups):
        slab = jnp.where(far, rows[(g + 1) % groups], rows[g])
        slab = jnp.where(lane < local, 0.5 * slab, slab)
        slabs.append(pltpu.roll(slab, g * local, 1) if g else slab)
    half = jnp.concatenate(slabs, axis=0)
    return half + half.T


def inverse_factor(inner):
    rank = inner.shape[0]
    row = lax.broadcasted_iota(jnp.int32, (rank, rank), 0)
    col = lax.broadcasted_iota(jnp.int32, (rank, rank), 1)
    work = jnp.concatenate([inner, jnp.where(row == col, 1.0, 0.0)], axis=1)
    shape = work.shape
    sub = lax.broadcasted_iota(jnp.int32, shape, 0)
    pivots = jnp.ones(shape, jnp.float32)
    for start in range(0, rank, PIVOTS):
        ks = range(start, start + PIVOTS)
        columns = [jnp.broadcast_to(work[:, k : k + 1], shape) for k in ks]
        lines = [work[k : k + 1, :] for k in ks]
        for j, k in enumerate(ks):
            pivot = columns[j][k : k + 1, :]
            pivots = jnp.where(sub == k, pivot, pivots)
            factor = jnp.where(sub > k, columns[j] * (1.0 / pivot), 0.0)
            for i in range(j + 1, PIVOTS):
                columns[i] = columns[i] - factor * columns[i][k : k + 1, :]
                lines[i] = lines[i] - factor[start + i : start + i + 1, :] * lines[j]
            work = work - factor * lines[j]
    return work[:, rank:] * lax.rsqrt(pivots[:, rank:])


def project_kernel(count, local, place_ref, raw_ref, start_ref, *refs):
    own_ref, *split_refs = refs[:7]
    out_ref, held, others, ready, in_sems, out_sems = refs[7:]
    height, cells = out_ref.shape
    tiles = cells // LANES
    group, ring, mirrored = (place_ref[i] for i in range(3))
    second = jnp.where(ring >= 2, 1, 0)
    later = jnp.where((ring == 1) | (ring == 2), 1, 0)
    fetches = tile_copies(own_ref, held, 0, in_sems, 0)
    ends = ((4 * mirrored, second), (2, later), (4 - 4 * mirrored, second))
    places = [others.at[at + end] for at, first in ends for end in (first, 1 - first)]
    for i, (block, place) in enumerate(zip(split_refs, places)):
        fetches += tile_copies(block, place, 0, in_sems, (1 + i) * tiles)
    for fetch in fetches:
        fetch.start()
    rank = start_ref.shape[0] - 1
    periods = start_ref.shape[1]
    groups = periods // local
    start = pltpu.roll(start_ref[...], lax.rem(periods - group * local, periods), 1)
    gain = start[rank:]
    per_period = height // local
    half = per_period // 2
    firsts = [pl.multiple_of(lax.rem(group + g, groups) * local, local) for g in range(groups)]
    raw = assemble([raw_ref[pl.ds(first, local), :] for first in firsts])

    def grow(basis):
        return dot(basis * gain, raw, 1, 0) * (gain * (1.0 / count))

    grown = grow(start[:rank])
    for _ in range(ITERS - 1):
        later = grow(grown)
        grown = dot(inverse_factor(dot(grown, grown, 1, 1)), later, 1, 0)
    basis = dot(inverse_factor(dot(grown, grown, 1, 1)), grown, 1, 0)
    high, low = halves(dot(basis[:, :local], basis * gain, 0, 0))
    mix = jnp.concatenate(
        [jnp.concatenate([high, high], axis=1), jnp.concatenate([low, jnp.zeros_like(low)], axis=1)],
        axis=0,
    )
    for fetch in fetches:
        fetch.wait()
    step = held.shape[0] // tiles
    side = others.shape[1] // tiles
    sends = []
    for pair in range(0, tiles, 2):
        for s in range(per_period):
            line = jnp.concatenate(
                [
                    jnp.concatenate(
                        [
                            held[pl.ds(c * step + s, local, stride=per_period), :],
                            *(
                                others[
                                    at + s // half, pl.ds(c * side + s % half, local, stride=half), :
                                ]
                                for at in (0, 2, 4)
                            ),
                        ],
                        axis=0,
                    )
                    for c in range(pair, pair + 2)
                ],
                axis=1,
            )
            result = dot(mix, jnp.concatenate(halves(line), axis=0), 1, 0, None)
            result = result[:local] + result[local:]
            for c in range(2):
                ready[pl.ds((pair + c) * height + s, local, stride=per_period), :] = result[
                    :, c * LANES : (c + 1) * LANES
                ]
        for c in range(pair, pair + 2):
            sends.append(
                pltpu.make_async_copy(
                    ready.at[pl.ds(c * height, height)],
                    out_ref.at[:, pl.ds(c * LANES, LANES)],
                    out_sems.at[c],
                )
            )
            sends[-1].start()
    for send in sends:
        send.wait()


def project(raw, start, place, blocks, local, count):
    height, cells = blocks[0].shape
    periods = start.shape[1]
    tiles = cells // LANES
    return pl.pallas_call(
        functools.partial(project_kernel, count, local),
        out_shape=jax.ShapeDtypeStruct((height, cells), jnp.float32),
        in_specs=[pl.BlockSpec(memory_space=pltpu.SMEM)] + [VMEM] * 2 + [ANY] * len(blocks),
        out_specs=ANY,
        scratch_shapes=[pltpu.VMEM((tiles * height, LANES), jnp.float32)]
        + [
            pltpu.VMEM((6, tiles * height // 2, LANES), jnp.float32),
            pltpu.VMEM((tiles * height, LANES), jnp.float32),
            pltpu.SemaphoreType.DMA((len(blocks) * tiles,)),
            pltpu.SemaphoreType.DMA((tiles,)),
        ],
        compiler_params=pltpu.CompilerParams(vmem_limit_bytes=32 * 2**20),
        name="project",
    )(place, raw, start, *blocks)


def shift(value, step):
    count = lax.axis_size("x")
    cores = lax.axis_size("c")
    pairs = [
        (c * count + i, c * count + (i + (step if c == 0 else -step)) % count)
        for c in range(cores)
        for i in range(count)
    ]
    return lax.ppermute(value, ("c", "x"), pairs)


def copies_of(pieces, count):
    piece = jnp.sum(pieces, 0)
    return lax.optimization_barrier(jnp.broadcast_to(piece[None], (count,) + piece.shape))


def per_device(field, gain, start_basis):
    groups = lax.axis_size("x")
    group = lax.axis_index("x")
    core = lax.axis_index("c")
    ring = jnp.where(core == 0, group, (groups - group) % groups)
    place = jnp.stack([group, ring, core]).astype(jnp.int32)
    local, parts, layers, cells = field.shape
    periods = gain.shape[0]
    pairs = lax.axis_size("y") * lax.axis_size("c")
    count = float(parts * layers * cells * lax.axis_size("z") * pairs)
    own = field.reshape(-1, cells)

    def side(block, part):
        part = lax.dynamic_index_in_dim(block.reshape(field.shape), part, 1, keepdims=False)
        return part.reshape(-1, cells)

    sent = (ring + groups - 1) % groups // 2
    start = jnp.concatenate([start_basis.T, gain[None]], axis=0)
    one = side(own, 1 - sent)
    source, one = lax.optimization_barrier((own, one))
    first = shift(one, 1)
    two = side(source, sent)
    after = shift(two, -1)
    second = shift(two, 1)
    first, start = lax.optimization_barrier((first, start))
    one, after, _ = lax.optimization_barrier((one, after, first))
    rest = [shift(one, -1), shift(after, -1), shift(first, 1)]
    gram = gram_of(place, own, [first, second, after], local, periods)
    pieces = lax.all_to_all(gram.reshape(pairs, -1, periods), PAIRS, 0, 0, tiled=True)
    copies = copies_of(pieces, lax.axis_size("z"))
    pieces = lax.all_to_all(copies, "z", 0, 0, tiled=True)
    copies, rest = lax.optimization_barrier((copies_of(pieces, groups * pairs), rest))
    raw = lax.all_to_all(copies, ("x",) + PAIRS, 0, 0, tiled=True).reshape(periods, periods)
    blocks = [own, after, *rest, first, second]
    result = project(raw, start, place, blocks, local, count)
    return result.reshape(field.shape)


def solution(mesh):
    cells, per = mesh.devices.shape
    split = Mesh(mesh.devices.reshape(4, cells // 8, 2, per), ("y", "z", "c", "x"))
    spec = P("x", None, None, ("y", "z", "c"))
    return jax.shard_map(
        per_device, mesh=split, in_specs=(spec, P(), P()), out_specs=spec, check_vma=False
    )
```

```python
import functools

import jax
import jax.numpy as jnp
from jax import lax
from jax.experimental import pallas as pl
from jax.experimental.pallas import tpu as pltpu
from jax.sharding import Mesh, PartitionSpec as P

ITERS = 3
PIVOTS = 16
LANES = 128
HIGH = lax.Precision.HIGHEST
PAIRS = ("y", "c")
VMEM = pl.BlockSpec(memory_space=pltpu.VMEM)
ANY = pl.BlockSpec(memory_space=pl.ANY)


def dot(a, b, ca, cb, precision=HIGH):
    return lax.dot_general(
        a, b, (((ca,), (cb,)), ((), ())), precision=precision, preferred_element_type=jnp.float32
    )


def halves(value):
    high = value.astype(jnp.bfloat16)
    return high, (value - high.astype(jnp.float32)).astype(jnp.bfloat16)


def tile_copies(block, held, first, sems, at):
    lanes = held.shape[1]
    tiles = block.shape[1] // lanes
    step = held.shape[0] // tiles
    return [
        pltpu.make_async_copy(
            block.at[:, pl.ds(c * lanes, lanes)],
            held.at[pl.ds(c * step + first, block.shape[0])],
            sems.at[at + c],
        )
        for c in range(tiles)
    ]


def lines(held, tiles, first, count, stride):
    step = held.shape[0] // tiles
    return jnp.concatenate(
        [held[pl.ds(c * step + first, count, stride=stride), :] for c in range(tiles)], axis=1
    )


def fold(acc, local, at):
    high = acc[:local, at : at + local] + acc[:local, at + local : at + 2 * local]
    low = acc[local:, at : at + local] + acc[local:, at + local : at + 2 * local]
    return high + low


def decode(place, groups):
    core = jnp.where(place >= groups, 1, 0)
    group = place - core * groups
    return group, jnp.where((core > 0) & (group > 0), groups - group, group), core


def gram_kernel(local, place_ref, own_ref, *refs):
    blocks, (out_ref, own, *held, sems) = refs[:3], refs[3:]
    tiles = own_ref.shape[1] // LANES
    copies = tile_copies(own_ref, own, 0, sems, 0)
    for i, block in enumerate(blocks):
        copies += tile_copies(block, held[i], 0, sems, (i + 1) * tiles)
    for copy in copies:
        copy.start()
    for copy in copies:
        copy.wait()
    per_period = own_ref.shape[0] // local
    half = per_period // 2
    _, ring, core = decode(place_ref[0], out_ref.shape[1] // local)
    second = ring >= 2
    mirrored = core > 0
    near, far = None, None
    for s in range(half):
        parts = [lines(own, tiles, s + t * half, local, per_period) for t in range(2)]
        parts = [jnp.where(second, parts[1 - t], parts[t]) for t in range(2)]
        first, other, after = (halves(lines(block, tiles, s, local, half)) for block in held)
        for part, before in zip(parts, (first, other)):
            mine = halves(part)
            both = jnp.concatenate(mine + before, axis=0)
            product = dot(jnp.concatenate(mine, axis=0), both, 1, 1, None)
            near = product if near is None else near + product
        product = dot(jnp.concatenate(first, axis=0), jnp.concatenate(after, axis=0), 1, 1, None)
        far = product if far is None else far + product
    far = fold(far, local, 0)
    side = fold(near, local, 2 * local)
    out_ref[...] = jnp.concatenate(
        [
            fold(near, local, 0),
            jnp.where(mirrored, side, 0.0),
            jnp.where(mirrored, far.T, far),
            jnp.where(mirrored, 0.0, side),
        ],
        axis=1,
    )


def gram_of(place, own, blocks, local, periods):
    shape = (own.shape[0] * own.shape[1] // LANES, LANES)
    tiles = own.shape[1] // LANES
    return pl.pallas_call(
        functools.partial(gram_kernel, local),
        out_shape=jax.ShapeDtypeStruct((local, periods), jnp.float32),
        in_specs=[pl.BlockSpec(memory_space=pltpu.SMEM)] + [ANY] * 4,
        out_specs=VMEM,
        scratch_shapes=[pltpu.VMEM(shape, jnp.float32)]
        + [pltpu.VMEM((shape[0] // 2, LANES), jnp.float32)] * 3
        + [pltpu.SemaphoreType.DMA((4 * tiles,))],
        compiler_params=pltpu.CompilerParams(vmem_limit_bytes=32 * 2**20),
        name="gram",
    )(place[None], own, *blocks)


def assemble(rows):
    groups = len(rows)
    local = rows[0].shape[0]
    lane = lax.broadcasted_iota(jnp.int32, rows[0].shape, 1)
    far = (lane >= 2 * local) & (lane < 3 * local)
    slabs = []
    for g in range(groups):
        slab = jnp.where(far, rows[(g + 1) % groups], rows[g])
        slab = jnp.where(lane < local, 0.5 * slab, slab)
        slabs.append(pltpu.roll(slab, g * local, 1) if g else slab)
    half = jnp.concatenate(slabs, axis=0)
    return half + half.T


def inverse_factor(inner):
    rank = inner.shape[0]
    row = lax.broadcasted_iota(jnp.int32, (rank, rank), 0)
    col = lax.broadcasted_iota(jnp.int32, (rank, rank), 1)
    work = jnp.concatenate([inner, jnp.where(row == col, 1.0, 0.0)], axis=1)
    shape = work.shape
    sub = lax.broadcasted_iota(jnp.int32, shape, 0)
    pivots = jnp.ones(shape, jnp.float32)
    for start in range(0, rank, PIVOTS):
        ks = range(start, start + PIVOTS)
        columns = [jnp.broadcast_to(work[:, k : k + 1], shape) for k in ks]
        lines = [work[k : k + 1, :] for k in ks]
        for j, k in enumerate(ks):
            pivot = columns[j][k : k + 1, :]
            pivots = jnp.where(sub == k, pivot, pivots)
            factor = jnp.where(sub > k, columns[j] * (1.0 / pivot), 0.0)
            for i in range(j + 1, PIVOTS):
                columns[i] = columns[i] - factor * columns[i][k : k + 1, :]
                lines[i] = lines[i] - factor[start + i : start + i + 1, :] * lines[j]
            work = work - factor * lines[j]
    return work[:, rank:] * lax.rsqrt(pivots[:, rank:])


def project_kernel(count, local, place_ref, raw_ref, start_ref, *refs):
    own_ref, *split_refs = refs[:7]
    out_ref, held, others, ready, in_sems, out_sems = refs[7:]
    height, cells = out_ref.shape
    tiles = cells // LANES
    group, ring, mirrored = decode(place_ref[0], start_ref.shape[1] // local)
    second = jnp.where(ring >= 2, 1, 0)
    later = jnp.where((ring == 1) | (ring == 2), 1, 0)
    fetches = tile_copies(own_ref, held, 0, in_sems, 0)
    ends = ((4 * mirrored, second), (2, later), (4 - 4 * mirrored, second))
    places = [others.at[at + end] for at, first in ends for end in (first, 1 - first)]
    for i, (block, place) in enumerate(zip(split_refs, places)):
        fetches += tile_copies(block, place, 0, in_sems, (1 + i) * tiles)
    for fetch in fetches:
        fetch.start()
    rank = start_ref.shape[0] - 1
    periods = start_ref.shape[1]
    groups = periods // local
    start = pltpu.roll(start_ref[...], lax.rem(periods - group * local, periods), 1)
    gain = start[rank:]
    per_period = height // local
    half = per_period // 2
    firsts = [pl.multiple_of(lax.rem(group + g, groups) * local, local) for g in range(groups)]
    raw = assemble([raw_ref[pl.ds(first, local), :] for first in firsts])

    def grow(basis):
        return dot(basis * gain, raw, 1, 0) * (gain * (1.0 / count))

    grown = grow(start[:rank])
    for _ in range(ITERS - 1):
        later = grow(grown)
        grown = dot(inverse_factor(dot(grown, grown, 1, 1)), later, 1, 0)
    basis = dot(inverse_factor(dot(grown, grown, 1, 1)), grown, 1, 0)
    high, low = halves(dot(basis[:, :local], basis * gain, 0, 0))
    mix = jnp.concatenate(
        [jnp.concatenate([high, high], axis=1), jnp.concatenate([low, jnp.zeros_like(low)], axis=1)],
        axis=0,
    )
    for fetch in fetches:
        fetch.wait()
    step = held.shape[0] // tiles
    side = others.shape[1] // tiles
    sends = []
    for pair in range(0, tiles, 2):
        for s in range(per_period):
            line = jnp.concatenate(
                [
                    jnp.concatenate(
                        [
                            held[pl.ds(c * step + s, local, stride=per_period), :],
                            *(
                                others[
                                    at + s // half, pl.ds(c * side + s % half, local, stride=half), :
                                ]
                                for at in (0, 2, 4)
                            ),
                        ],
                        axis=0,
                    )
                    for c in range(pair, pair + 2)
                ],
                axis=1,
            )
            result = dot(mix, jnp.concatenate(halves(line), axis=0), 1, 0, None)
            result = result[:local] + result[local:]
            for c in range(2):
                ready[pl.ds((pair + c) * height + s, local, stride=per_period), :] = result[
                    :, c * LANES : (c + 1) * LANES
                ]
        for c in range(pair, pair + 2):
            sends.append(
                pltpu.make_async_copy(
                    ready.at[pl.ds(c * height, height)],
                    out_ref.at[:, pl.ds(c * LANES, LANES)],
                    out_sems.at[c],
                )
            )
            sends[-1].start()
    for send in sends:
        send.wait()


def project(raw, start, place, blocks, local, count):
    height, cells = blocks[0].shape
    periods = start.shape[1]
    tiles = cells // LANES
    return pl.pallas_call(
        functools.partial(project_kernel, count, local),
        out_shape=jax.ShapeDtypeStruct((height, cells), jnp.float32),
        in_specs=[pl.BlockSpec(memory_space=pltpu.SMEM)] + [VMEM] * 2 + [ANY] * len(blocks),
        out_specs=ANY,
        scratch_shapes=[pltpu.VMEM((tiles * height, LANES), jnp.float32)]
        + [
            pltpu.VMEM((6, tiles * height // 2, LANES), jnp.float32),
            pltpu.VMEM((tiles * height, LANES), jnp.float32),
            pltpu.SemaphoreType.DMA((len(blocks) * tiles,)),
            pltpu.SemaphoreType.DMA((tiles,)),
        ],
        compiler_params=pltpu.CompilerParams(vmem_limit_bytes=32 * 2**20),
        name="project",
    )(place[None], raw, start, *blocks)


def shift(value, step):
    count = lax.axis_size("x")
    cores = lax.axis_size("c")
    pairs = [
        (c * count + i, c * count + (i + (step if c == 0 else -step)) % count)
        for c in range(cores)
        for i in range(count)
    ]
    return lax.ppermute(value, ("c", "x"), pairs)


def copies_of(pieces, count):
    piece = jnp.sum(pieces, 0)
    return lax.optimization_barrier(jnp.broadcast_to(piece[None], (count,) + piece.shape))


def per_device(field, gain, start_basis):
    groups = lax.axis_size("x")
    group = lax.axis_index("x")
    core = lax.axis_index("c")
    place = core * groups + group
    ring = decode(place, groups)[1]
    local, parts, layers, cells = field.shape
    periods = gain.shape[0]
    pairs = lax.axis_size("y") * lax.axis_size("c")
    count = float(parts * layers * cells * lax.axis_size("z") * pairs)
    own = field.reshape(-1, cells)

    def side(block, part):
        part = lax.dynamic_index_in_dim(block.reshape(field.shape), part, 1, keepdims=False)
        return part.reshape(-1, cells)

    sent = (ring + groups - 1) % groups // 2
    start = jnp.concatenate([start_basis.T, gain[None]], axis=0)
    one = side(own, 1 - sent)
    source, one = lax.optimization_barrier((own, one))
    first = shift(one, 1)
    two = side(source, sent)
    after = shift(two, -1)
    second = shift(two, 1)
    first, start = lax.optimization_barrier((first, start))
    one, first = lax.optimization_barrier((one, first))
    rest = [shift(one, -1), shift(after, -1), shift(first, 1)]
    gram = gram_of(place, own, [first, second, after], local, periods)
    pieces = lax.all_to_all(gram.reshape(pairs, -1, periods), PAIRS, 0, 0, tiled=True)
    copies = copies_of(pieces, lax.axis_size("z"))
    pieces = lax.all_to_all(copies, "z", 0, 0, tiled=True)
    copies, rest = lax.optimization_barrier((copies_of(pieces, groups * pairs), rest))
    raw = lax.all_to_all(copies, ("x",) + PAIRS, 0, 0, tiled=True).reshape(periods, periods)
    blocks = [own, after, *rest, first, second]
    result = project(raw, start, place, blocks, local, count)
    return result.reshape(field.shape)


def solution(mesh):
    cells, per = mesh.devices.shape
    split = Mesh(mesh.devices.reshape(4, cells // 8, 2, per), ("y", "z", "c", "x"))
    spec = P("x", None, None, ("y", "z", "c"))
    return jax.shard_map(
        per_device, mesh=split, in_specs=(spec, P(), P()), out_specs=spec, check_vma=False
    )
```

```python
import functools

import jax
import jax.numpy as jnp
from jax import lax
from jax.experimental import pallas as pl
from jax.experimental.pallas import tpu as pltpu
from jax.sharding import Mesh, PartitionSpec as P

ITERS = 3
PIVOTS = 16
LANES = 128
HIGH = lax.Precision.HIGHEST
PAIRS = ("y", "c")
VMEM = pl.BlockSpec(memory_space=pltpu.VMEM)
ANY = pl.BlockSpec(memory_space=pl.ANY)


def dot(a, b, ca, cb, precision=HIGH):
    return lax.dot_general(
        a, b, (((ca,), (cb,)), ((), ())), precision=precision, preferred_element_type=jnp.float32
    )


def halves(value):
    high = value.astype(jnp.bfloat16)
    return high, (value - high.astype(jnp.float32)).astype(jnp.bfloat16)


def tile_copies(block, held, first, sems, at):
    lanes = held.shape[1]
    tiles = block.shape[1] // lanes
    step = held.shape[0] // tiles
    return [
        pltpu.make_async_copy(
            block.at[:, pl.ds(c * lanes, lanes)],
            held.at[pl.ds(c * step + first, block.shape[0])],
            sems.at[at + c],
        )
        for c in range(tiles)
    ]


def lines(held, tiles, first, count, stride):
    step = held.shape[0] // tiles
    return jnp.concatenate(
        [held[pl.ds(c * step + first, count, stride=stride), :] for c in range(tiles)], axis=1
    )


def fold(acc, local, at):
    high = acc[:local, at : at + local] + acc[:local, at + local : at + 2 * local]
    low = acc[local:, at : at + local] + acc[local:, at + local : at + 2 * local]
    return high + low


def decode(place, groups):
    core = jnp.where(place >= groups, 1, 0)
    group = place - core * groups
    return group, jnp.where((core > 0) & (group > 0), groups - group, group), core


def gram_kernel(local, place_ref, own_ref, *refs):
    blocks, (out_ref, own, *held, sems) = refs[:3], refs[3:]
    tiles = own_ref.shape[1] // LANES
    copies = tile_copies(own_ref, own, 0, sems, 0)
    for i, block in enumerate(blocks):
        copies += tile_copies(block, held[i], 0, sems, (i + 1) * tiles)
    for copy in copies:
        copy.start()
    for copy in copies:
        copy.wait()
    per_period = own_ref.shape[0] // local
    half = per_period // 2
    _, ring, core = decode(place_ref[0], out_ref.shape[1] // local)
    second = ring >= 2
    mirrored = core > 0
    near, far = None, None
    for s in range(half):
        parts = [lines(own, tiles, s + t * half, local, per_period) for t in range(2)]
        parts = [jnp.where(second, parts[1 - t], parts[t]) for t in range(2)]
        first, other, after = (halves(lines(block, tiles, s, local, half)) for block in held)
        for part, before in zip(parts, (first, other)):
            mine = halves(part)
            both = jnp.concatenate(mine + before, axis=0)
            product = dot(jnp.concatenate(mine, axis=0), both, 1, 1, None)
            near = product if near is None else near + product
        product = dot(jnp.concatenate(first, axis=0), jnp.concatenate(after, axis=0), 1, 1, None)
        far = product if far is None else far + product
    far = fold(far, local, 0)
    side = fold(near, local, 2 * local)
    out_ref[...] = jnp.concatenate(
        [
            fold(near, local, 0),
            jnp.where(mirrored, side, 0.0),
            jnp.where(mirrored, far.T, far),
            jnp.where(mirrored, 0.0, side),
        ],
        axis=1,
    )


def gram_of(place, own, blocks, local, periods):
    shape = (own.shape[0] * own.shape[1] // LANES, LANES)
    tiles = own.shape[1] // LANES
    return pl.pallas_call(
        functools.partial(gram_kernel, local),
        out_shape=jax.ShapeDtypeStruct((local, periods), jnp.float32),
        in_specs=[pl.BlockSpec(memory_space=pltpu.SMEM)] + [ANY] * 4,
        out_specs=VMEM,
        scratch_shapes=[pltpu.VMEM(shape, jnp.float32)]
        + [pltpu.VMEM((shape[0] // 2, LANES), jnp.float32)] * 3
        + [pltpu.SemaphoreType.DMA((4 * tiles,))],
        compiler_params=pltpu.CompilerParams(vmem_limit_bytes=32 * 2**20),
        name="gram",
    )(place[None], own, *blocks)


def assemble(rows):
    groups = len(rows)
    local = rows[0].shape[0]
    lane = lax.broadcasted_iota(jnp.int32, rows[0].shape, 1)
    far = (lane >= 2 * local) & (lane < 3 * local)
    slabs = []
    for g in range(groups):
        slab = jnp.where(far, rows[(g + 1) % groups], rows[g])
        slab = jnp.where(lane < local, 0.5 * slab, slab)
        slabs.append(pltpu.roll(slab, g * local, 1) if g else slab)
    half = jnp.concatenate(slabs, axis=0)
    return half + half.T


def inverse_factor(inner):
    rank = inner.shape[0]
    row = lax.broadcasted_iota(jnp.int32, (rank, rank), 0)
    col = lax.broadcasted_iota(jnp.int32, (rank, rank), 1)
    work = jnp.concatenate([inner, jnp.where(row == col, 1.0, 0.0)], axis=1)
    shape = work.shape
    sub = lax.broadcasted_iota(jnp.int32, shape, 0)
    pivots = jnp.ones(shape, jnp.float32)
    for start in range(0, rank, PIVOTS):
        ks = range(start, start + PIVOTS)
        columns = [jnp.broadcast_to(work[:, k : k + 1], shape) for k in ks]
        lines = [work[k : k + 1, :] for k in ks]
        for j, k in enumerate(ks):
            pivot = columns[j][k : k + 1, :]
            pivots = jnp.where(sub == k, pivot, pivots)
            factor = jnp.where(sub > k, columns[j] * (1.0 / pivot), 0.0)
            for i in range(j + 1, PIVOTS):
                columns[i] = columns[i] - factor * columns[i][k : k + 1, :]
                lines[i] = lines[i] - factor[start + i : start + i + 1, :] * lines[j]
            work = work - factor * lines[j]
    return work[:, rank:] * lax.rsqrt(pivots[:, rank:])


def project_kernel(count, local, place_ref, raw_ref, start_ref, *refs):
    own_ref, *split_refs = refs[:7]
    out_ref, held, others, ready, in_sems, out_sems = refs[7:]
    height, cells = out_ref.shape
    tiles = cells // LANES
    group, ring, mirrored = decode(place_ref[0], start_ref.shape[1] // local)
    second = jnp.where(ring >= 2, 1, 0)
    later = jnp.where((ring == 1) | (ring == 2), 1, 0)
    fetches = tile_copies(own_ref, held, 0, in_sems, 0)
    ends = ((4 * mirrored, second), (2, later), (4 - 4 * mirrored, second))
    places = [others.at[at + end] for at, first in ends for end in (first, 1 - first)]
    for i, (block, place) in enumerate(zip(split_refs, places)):
        fetches += tile_copies(block, place, 0, in_sems, (1 + i) * tiles)
    for fetch in fetches:
        fetch.start()
    rank = start_ref.shape[0] - 1
    periods = start_ref.shape[1]
    groups = periods // local
    start = pltpu.roll(start_ref[...], lax.rem(periods - group * local, periods), 1)
    gain = start[rank:]
    per_period = height // local
    half = per_period // 2
    firsts = [pl.multiple_of(lax.rem(group + g, groups) * local, local) for g in range(groups)]
    raw = assemble([raw_ref[pl.ds(first, local), :] for first in firsts])

    def grow(basis):
        return dot(basis * gain, raw, 1, 0) * (gain * (1.0 / count))

    grown = grow(start[:rank])
    for _ in range(ITERS - 1):
        later = grow(grown)
        grown = dot(inverse_factor(dot(grown, grown, 1, 1)), later, 1, 0)
    basis = dot(inverse_factor(dot(grown, grown, 1, 1)), grown, 1, 0)
    high, low = halves(dot(basis[:, :local], basis * gain, 0, 0))
    mix = jnp.concatenate(
        [jnp.concatenate([high, high], axis=1), jnp.concatenate([low, jnp.zeros_like(low)], axis=1)],
        axis=0,
    )
    for fetch in fetches:
        fetch.wait()
    step = held.shape[0] // tiles
    side = others.shape[1] // tiles
    sends = []
    for pair in range(0, tiles, 2):
        for s in range(per_period):
            line = jnp.concatenate(
                [
                    jnp.concatenate(
                        [
                            held[pl.ds(c * step + s, local, stride=per_period), :],
                            *(
                                others[
                                    at + s // half, pl.ds(c * side + s % half, local, stride=half), :
                                ]
                                for at in (0, 2, 4)
                            ),
                        ],
                        axis=0,
                    )
                    for c in range(pair, pair + 2)
                ],
                axis=1,
            )
            result = dot(mix, jnp.concatenate(halves(line), axis=0), 1, 0, None)
            result = result[:local] + result[local:]
            for c in range(2):
                ready[pl.ds((pair + c) * height + s, local, stride=per_period), :] = result[
                    :, c * LANES : (c + 1) * LANES
                ]
        for c in range(pair, pair + 2):
            sends.append(
                pltpu.make_async_copy(
                    ready.at[pl.ds(c * height, height)],
                    out_ref.at[:, pl.ds(c * LANES, LANES)],
                    out_sems.at[c],
                )
            )
            sends[-1].start()
    for send in sends:
        send.wait()


def project(raw, start, place, blocks, local, count):
    height, cells = blocks[0].shape
    periods = start.shape[1]
    tiles = cells // LANES
    return pl.pallas_call(
        functools.partial(project_kernel, count, local),
        out_shape=jax.ShapeDtypeStruct((height, cells), jnp.float32),
        in_specs=[pl.BlockSpec(memory_space=pltpu.SMEM)] + [VMEM] * 2 + [ANY] * len(blocks),
        out_specs=ANY,
        scratch_shapes=[pltpu.VMEM((tiles * height, LANES), jnp.float32)]
        + [
            pltpu.VMEM((6, tiles * height // 2, LANES), jnp.float32),
            pltpu.VMEM((tiles * height, LANES), jnp.float32),
            pltpu.SemaphoreType.DMA((len(blocks) * tiles,)),
            pltpu.SemaphoreType.DMA((tiles,)),
        ],
        compiler_params=pltpu.CompilerParams(vmem_limit_bytes=32 * 2**20),
        name="project",
    )(place[None], raw, start, *blocks)


def shift(value, step):
    count = lax.axis_size("x")
    cores = lax.axis_size("c")
    pairs = [
        (c * count + i, c * count + (i + (step if c == 0 else -step)) % count)
        for c in range(cores)
        for i in range(count)
    ]
    return lax.ppermute(value, ("c", "x"), pairs)


def copies_of(pieces, count):
    piece = jnp.sum(pieces, 0)
    return lax.optimization_barrier(jnp.broadcast_to(piece[None], (count,) + piece.shape))


def per_device(field, gain, start_basis):
    groups = lax.axis_size("x")
    group = lax.axis_index("x")
    core = lax.axis_index("c")
    place = core * groups + group
    ring = decode(place, groups)[1]
    local, parts, layers, cells = field.shape
    periods = gain.shape[0]
    pairs = lax.axis_size("y") * lax.axis_size("c")
    count = float(parts * layers * cells * lax.axis_size("z") * pairs)
    own = field.reshape(-1, cells)

    def side(block, part):
        part = lax.dynamic_index_in_dim(block.reshape(field.shape), part, 1, keepdims=False)
        return part.reshape(-1, cells)

    sent = (ring + groups - 1) % groups // 2
    start = jnp.concatenate([start_basis.T, gain[None]], axis=0)
    one = side(own, 1 - sent)
    source, one = lax.optimization_barrier((own, one))
    first = shift(one, 1)
    two = side(source, sent)
    after = shift(two, -1)
    second = shift(two, 1)
    first, start = lax.optimization_barrier((first, start))
    one, first = lax.optimization_barrier((one, first))
    rest = [shift(one, -1), shift(after, -1), shift(first, 1)]
    gram = gram_of(place, own, [first, second, after], local, periods)
    pieces = lax.all_to_all(gram.reshape(pairs, -1, periods), PAIRS, 0, 0, tiled=True)
    copies, rest[0], rest[2] = lax.optimization_barrier(
        (copies_of(pieces, lax.axis_size("z")), rest[0], rest[2])
    )
    pieces = lax.all_to_all(copies, "z", 0, 0, tiled=True)
    copies, rest = lax.optimization_barrier((copies_of(pieces, groups * pairs), rest))
    raw = lax.all_to_all(copies, ("x",) + PAIRS, 0, 0, tiled=True).reshape(periods, periods)
    blocks = [own, after, *rest, first, second]
    result = project(raw, start, place, blocks, local, count)
    return result.reshape(field.shape)


def solution(mesh):
    cells, per = mesh.devices.shape
    split = Mesh(mesh.devices.reshape(4, cells // 8, 2, per), ("y", "z", "c", "x"))
    spec = P("x", None, None, ("y", "z", "c"))
    return jax.shard_map(
        per_device, mesh=split, in_specs=(spec, P(), P()), out_specs=spec, check_vma=False
    )
```

```python
import functools

import jax
import jax.numpy as jnp
from jax import lax
from jax.experimental import pallas as pl
from jax.experimental.pallas import tpu as pltpu
from jax.sharding import Mesh, PartitionSpec as P

ITERS = 3
PIVOTS = 16
LANES = 128
HIGH = lax.Precision.HIGHEST
PAIRS = ("y", "c")
VMEM = pl.BlockSpec(memory_space=pltpu.VMEM)
ANY = pl.BlockSpec(memory_space=pl.ANY)


def dot(a, b, ca, cb, precision=HIGH):
    return lax.dot_general(
        a, b, (((ca,), (cb,)), ((), ())), precision=precision, preferred_element_type=jnp.float32
    )


def halves(value):
    high = value.astype(jnp.bfloat16)
    return high, (value - high.astype(jnp.float32)).astype(jnp.bfloat16)


def tile_copies(block, held, first, sems, at):
    lanes = held.shape[1]
    tiles = block.shape[1] // lanes
    step = held.shape[0] // tiles
    return [
        pltpu.make_async_copy(
            block.at[:, pl.ds(c * lanes, lanes)],
            held.at[pl.ds(c * step + first, block.shape[0])],
            sems.at[at + c],
        )
        for c in range(tiles)
    ]


def lines(held, tiles, first, count, stride):
    step = held.shape[0] // tiles
    return jnp.concatenate(
        [held[pl.ds(c * step + first, count, stride=stride), :] for c in range(tiles)], axis=1
    )


def fold(acc, local, at):
    high = acc[:local, at : at + local] + acc[:local, at + local : at + 2 * local]
    low = acc[local:, at : at + local] + acc[local:, at + local : at + 2 * local]
    return high + low


def decode(place, groups):
    core = jnp.where(place >= groups, 1, 0)
    group = place - core * groups
    return group, jnp.where((core > 0) & (group > 0), groups - group, group), core


def gram_kernel(local, place_ref, own_ref, *refs):
    blocks, (out_ref, own, *held, sems) = refs[:3], refs[3:]
    tiles = own_ref.shape[1] // LANES
    copies = tile_copies(own_ref, own, 0, sems, 0)
    for i, block in enumerate(blocks):
        copies += tile_copies(block, held[i], 0, sems, (i + 1) * tiles)
    for copy in copies:
        copy.start()
    for copy in copies:
        copy.wait()
    per_period = own_ref.shape[0] // local
    half = per_period // 2
    _, ring, core = decode(place_ref[0], out_ref.shape[1] // local)
    second = ring >= 2
    mirrored = core > 0
    near, far = None, None
    for s in range(half):
        parts = [lines(own, tiles, s + t * half, local, per_period) for t in range(2)]
        parts = [jnp.where(second, parts[1 - t], parts[t]) for t in range(2)]
        first, other, after = (halves(lines(block, tiles, s, local, half)) for block in held)
        for part, before in zip(parts, (first, other)):
            mine = halves(part)
            both = jnp.concatenate(mine + before, axis=0)
            product = dot(jnp.concatenate(mine, axis=0), both, 1, 1, None)
            near = product if near is None else near + product
        product = dot(jnp.concatenate(first, axis=0), jnp.concatenate(after, axis=0), 1, 1, None)
        far = product if far is None else far + product
    far = fold(far, local, 0)
    side = fold(near, local, 2 * local)
    out_ref[...] = jnp.concatenate(
        [
            fold(near, local, 0),
            jnp.where(mirrored, side, 0.0),
            jnp.where(mirrored, far.T, far),
            jnp.where(mirrored, 0.0, side),
        ],
        axis=1,
    )


def gram_of(place, own, blocks, local, periods):
    shape = (own.shape[0] * own.shape[1] // LANES, LANES)
    tiles = own.shape[1] // LANES
    return pl.pallas_call(
        functools.partial(gram_kernel, local),
        out_shape=jax.ShapeDtypeStruct((local, periods), jnp.float32),
        in_specs=[pl.BlockSpec(memory_space=pltpu.SMEM)] + [ANY] * 4,
        out_specs=VMEM,
        scratch_shapes=[pltpu.VMEM(shape, jnp.float32)]
        + [pltpu.VMEM((shape[0] // 2, LANES), jnp.float32)] * 3
        + [pltpu.SemaphoreType.DMA((4 * tiles,))],
        compiler_params=pltpu.CompilerParams(vmem_limit_bytes=32 * 2**20),
        name="gram",
    )(place[None], own, *blocks)


def assemble(rows):
    groups = len(rows)
    local = rows[0].shape[0]
    lane = lax.broadcasted_iota(jnp.int32, rows[0].shape, 1)
    far = (lane >= 2 * local) & (lane < 3 * local)
    slabs = []
    for g in range(groups):
        slab = jnp.where(far, rows[(g + 1) % groups], rows[g])
        slab = jnp.where(lane < local, 0.5 * slab, slab)
        slabs.append(pltpu.roll(slab, g * local, 1) if g else slab)
    half = jnp.concatenate(slabs, axis=0)
    return half + half.T


def inverse_factor(inner):
    rank = inner.shape[0]
    row = lax.broadcasted_iota(jnp.int32, (rank, rank), 0)
    col = lax.broadcasted_iota(jnp.int32, (rank, rank), 1)
    work = jnp.concatenate([inner, jnp.where(row == col, 1.0, 0.0)], axis=1)
    shape = work.shape
    sub = lax.broadcasted_iota(jnp.int32, shape, 0)
    pivots = jnp.ones(shape, jnp.float32)
    for start in range(0, rank, PIVOTS):
        ks = range(start, start + PIVOTS)
        columns = [jnp.broadcast_to(work[:, k : k + 1], shape) for k in ks]
        lines = [work[k : k + 1, :] for k in ks]
        for j, k in enumerate(ks):
            pivot = columns[j][k : k + 1, :]
            pivots = jnp.where(sub == k, pivot, pivots)
            factor = jnp.where(sub > k, columns[j] * (1.0 / pivot), 0.0)
            for i in range(j + 1, PIVOTS):
                columns[i] = columns[i] - factor * columns[i][k : k + 1, :]
                lines[i] = lines[i] - factor[start + i : start + i + 1, :] * lines[j]
            work = work - factor * lines[j]
    return work[:, rank:] * lax.rsqrt(pivots[:, rank:])


def project_kernel(count, local, place_ref, raw_ref, start_ref, *refs):
    own_ref, *split_refs = refs[:7]
    out_ref, held, others, ready, in_sems, out_sems = refs[7:]
    height, cells = out_ref.shape
    tiles = cells // LANES
    group, ring, mirrored = decode(place_ref[0], start_ref.shape[1] // local)
    second = jnp.where(ring >= 2, 1, 0)
    later = jnp.where((ring == 1) | (ring == 2), 1, 0)
    fetches = tile_copies(own_ref, held, 0, in_sems, 0)
    ends = ((4 * mirrored, second), (2, later), (4 - 4 * mirrored, second))
    places = [others.at[at + end] for at, first in ends for end in (first, 1 - first)]
    for i, (block, place) in enumerate(zip(split_refs, places)):
        fetches += tile_copies(block, place, 0, in_sems, (1 + i) * tiles)
    for fetch in fetches:
        fetch.start()
    rank = start_ref.shape[0] - 1
    periods = start_ref.shape[1]
    groups = periods // local
    start = pltpu.roll(start_ref[...], lax.rem(periods - group * local, periods), 1)
    gain = start[rank:]
    per_period = height // local
    half = per_period // 2
    firsts = [pl.multiple_of(lax.rem(group + g, groups) * local, local) for g in range(groups)]
    raw = assemble([raw_ref[pl.ds(first, local), :] for first in firsts])

    def grow(basis):
        return dot(basis * gain, raw, 1, 0) * (gain * (1.0 / count))

    grown = grow(start[:rank])
    for _ in range(ITERS - 1):
        later = grow(grown)
        grown = dot(inverse_factor(dot(grown, grown, 1, 1)), later, 1, 0)
    basis = dot(inverse_factor(dot(grown, grown, 1, 1)), grown, 1, 0)
    high, low = halves(dot(basis[:, :local], basis * gain, 0, 0))
    mix = jnp.concatenate(
        [jnp.concatenate([high, high], axis=1), jnp.concatenate([low, jnp.zeros_like(low)], axis=1)],
        axis=0,
    )
    for fetch in fetches:
        fetch.wait()
    step = held.shape[0] // tiles
    side = others.shape[1] // tiles
    sends = []
    for pair in range(0, tiles, 2):
        for s in range(per_period):
            line = jnp.concatenate(
                [
                    jnp.concatenate(
                        [
                            held[pl.ds(c * step + s, local, stride=per_period), :],
                            *(
                                others[
                                    at + s // half, pl.ds(c * side + s % half, local, stride=half), :
                                ]
                                for at in (0, 2, 4)
                            ),
                        ],
                        axis=0,
                    )
                    for c in range(pair, pair + 2)
                ],
                axis=1,
            )
            result = dot(mix, jnp.concatenate(halves(line), axis=0), 1, 0, None)
            result = result[:local] + result[local:]
            for c in range(2):
                ready[pl.ds((pair + c) * height + s, local, stride=per_period), :] = result[
                    :, c * LANES : (c + 1) * LANES
                ]
        for c in range(pair, pair + 2):
            sends.append(
                pltpu.make_async_copy(
                    ready.at[pl.ds(c * height, height)],
                    out_ref.at[:, pl.ds(c * LANES, LANES)],
                    out_sems.at[c],
                )
            )
            sends[-1].start()
    for send in sends:
        send.wait()


def project(raw, start, place, blocks, local, count):
    height, cells = blocks[0].shape
    periods = start.shape[1]
    tiles = cells // LANES
    return pl.pallas_call(
        functools.partial(project_kernel, count, local),
        out_shape=jax.ShapeDtypeStruct((height, cells), jnp.float32),
        in_specs=[pl.BlockSpec(memory_space=pltpu.SMEM)] + [VMEM] * 2 + [ANY] * len(blocks),
        out_specs=ANY,
        scratch_shapes=[pltpu.VMEM((tiles * height, LANES), jnp.float32)]
        + [
            pltpu.VMEM((6, tiles * height // 2, LANES), jnp.float32),
            pltpu.VMEM((tiles * height, LANES), jnp.float32),
            pltpu.SemaphoreType.DMA((len(blocks) * tiles,)),
            pltpu.SemaphoreType.DMA((tiles,)),
        ],
        compiler_params=pltpu.CompilerParams(vmem_limit_bytes=32 * 2**20),
        name="project",
    )(place[None], raw, start, *blocks)


def shift(value, step):
    count = lax.axis_size("x")
    cores = lax.axis_size("c")
    pairs = [
        (c * count + i, c * count + (i + (step if c == 0 else -step)) % count)
        for c in range(cores)
        for i in range(count)
    ]
    return lax.ppermute(value, ("c", "x"), pairs)


def copies_of(pieces, count):
    piece = jnp.sum(pieces, 0)
    return lax.optimization_barrier(jnp.broadcast_to(piece[None], (count,) + piece.shape))


def per_device(field, gain, start_basis):
    groups = lax.axis_size("x")
    group = lax.axis_index("x")
    core = lax.axis_index("c")
    place = core * groups + group
    ring = decode(place, groups)[1]
    local, parts, layers, cells = field.shape
    periods = gain.shape[0]
    pairs = lax.axis_size("y") * lax.axis_size("c")
    count = float(parts * layers * cells * lax.axis_size("z") * pairs)
    own = field.reshape(-1, cells)

    def side(block, part):
        part = lax.dynamic_index_in_dim(block.reshape(field.shape), part, 1, keepdims=False)
        return part.reshape(-1, cells)

    sent = (ring + groups - 1) % groups // 2
    start = jnp.concatenate([start_basis.T, gain[None]], axis=0)
    one = side(own, 1 - sent)
    source, one = lax.optimization_barrier((own, one))
    first = shift(one, 1)
    two = side(source, sent)
    after = shift(two, -1)
    second = shift(two, 1)
    first, start = lax.optimization_barrier((first, start))
    one, first = lax.optimization_barrier((one, first))
    rest = [shift(one, -1), shift(after, -1), shift(first, 1)]
    gram = gram_of(place, own, [first, second, after], local, periods)
    pieces = lax.all_to_all(gram.reshape(pairs, -1, periods), PAIRS, 0, 0, tiled=True)
    copies, rest[2] = lax.optimization_barrier((copies_of(pieces, lax.axis_size("z")), rest[2]))
    pieces = lax.all_to_all(copies, "z", 0, 0, tiled=True)
    copies, rest = lax.optimization_barrier((copies_of(pieces, groups * pairs), rest))
    raw = lax.all_to_all(copies, ("x",) + PAIRS, 0, 0, tiled=True).reshape(periods, periods)
    blocks = [own, after, *rest, first, second]
    result = project(raw, start, place, blocks, local, count)
    return result.reshape(field.shape)


def solution(mesh):
    cells, per = mesh.devices.shape
    split = Mesh(mesh.devices.reshape(4, cells // 8, 2, per), ("y", "z", "c", "x"))
    spec = P("x", None, None, ("y", "z", "c"))
    return jax.shard_map(
        per_device, mesh=split, in_specs=(spec, P(), P()), out_specs=spec, check_vma=False
    )
```
